128 devices in a mesh: seq: 8 (over z_hi, y), ctx: 16 (over z_lo, x, core).
Axes of the slice: x: 4, y: 4, z: 4 (z_hi: 2, z_lo: 2; z = z_hi * 2 + z_lo), core: 2. Of those that a mesh axis runs over, the one named last changes fastest.
Arguments:
- queries: bfloat16 [8, 2048, 4096], P('seq', 'ctx'), may hold values from -6 to 6
- keys_in: bfloat16 [8, 2048, 4096], P('seq', 'ctx'), may hold values from -6 to 6
- value_in: bfloat16 [8, 2048, 4096], P('seq', 'ctx'), may hold values from -6 to 6
- upstream: bfloat16 [8, 2048, 4096], P('seq', 'ctx'), may hold values from -6 to 6
- filter_taps: float32 [2048, 4096], P(None, 'ctx'), may hold values from -0.125 to 0.125
Outputs:
- query_grad: bfloat16 [8, 2048, 4096], P('seq', 'ctx')
- key_grad: bfloat16 [8, 2048, 4096], P('seq', 'ctx')
- value_grad: bfloat16 [8, 2048, 4096], P('seq', 'ctx')
- filter_grad: float32 [2048, 4096], P(None, 'ctx')
The draws below stay inside these ranges and needn't reach their ends.
All inputs are finite; a program needn't handle non-finite values.
Results may differ from the reference program's by a relative error of at most 0.009.
Values may be sent and summed in bfloat16 or wider, within the bound.
No kernel may reach another device: no remote copies, remote signals or barrier semaphores. Data moves between devices by JAX's collectives and lax.ppermute only.
A program may use at most 192 MiB of HBM per device.

```python
import math
import jax
import jax.numpy as jnp
from jax import lax

D = 4096
LEN = 2048
SEQS = 8


def block_scale(rng, extent, shards, smallest, high):
    factor_of = 1.0
    for axis_at, blocks in shards:
        heights = jax.random.uniform(jax.random.fold_in(jax.random.fold_in(rng, 6), axis_at), (blocks,), jnp.float32, smallest / len(shards), high / len(shards))
        factor_of = factor_of * jnp.repeat(jnp.exp(heights), extent[axis_at] // blocks).reshape((-1,) + (1,) * (len(extent) - 1 - axis_at))
    return factor_of


def scatter_about(stream_key, dims, spread, most, shards=(), kind=jnp.bfloat16):
    values = jax.random.normal(stream_key, dims, jnp.float32) * spread
    if len(shards) > 0:
        values = block_scale(stream_key, dims, shards, -0.22, 0.18) * values
    return jnp.clip(values, min=-most, max=most).astype(kind)


def setup_inputs(seed: int = 0) -> dict:
    splits = jax.random.split(jax.random.key(seed), 6)
    return {
        "queries": scatter_about(splits[0], (SEQS, LEN, D), 1.0, 6.0, ((0, 8), (1, 16))),
        "keys_in": scatter_about(splits[1], (SEQS, LEN, D), 1.0, 6.0, ((0, 8), (1, 16))),
        "value_in": scatter_about(splits[2], (SEQS, LEN, D), 1.0, 6.0, ((0, 8), (1, 16))),
        "upstream": scatter_about(splits[3], (SEQS, LEN, D), 1.0, 6.0, ((0, 8), (1, 16))),
        "filter_taps": scatter_about(splits[4], (LEN, D), LEN ** -0.5, 0.125, ((1, 16),), jnp.float32),
    }


def block_grads(pieces):
    queries, keys_in, value_in, upstream, tap_block = pieces
    seq_count = queries.shape[0]
    length = queries.shape[1]
    padded = 2 * length
    key_value = (keys_in.astype(jnp.float32) * value_in.astype(jnp.float32)).astype(jnp.bfloat16)
    key_wide = lax.optimization_barrier(key_value).astype(jnp.float32)
    gated_grad = (upstream.astype(jnp.float32) * queries.astype(jnp.float32)).astype(jnp.bfloat16)
    gated_wide = lax.optimization_barrier(gated_grad).astype(jnp.float32)
    spec_value = jnp.fft.rfft(key_wide, padded, axis=1)
    spec_grad = jnp.fft.rfft(gated_wide, padded, axis=1)
    spec_filter = jnp.fft.rfft(tap_block, padded, axis=0)[None]
    conv_out = jnp.fft.irfft(spec_value * spec_filter, padded, axis=1)[:, :length].astype(jnp.bfloat16)
    conv_grad = jnp.fft.irfft(spec_grad * jnp.conj(spec_filter), padded, axis=1)[:, :length].astype(jnp.bfloat16)
    cross = jnp.fft.irfft(spec_grad * jnp.conj(spec_value), padded, axis=1)[:, :length]
    filter_grad = lax.optimization_barrier(jnp.sum(cross, axis=0)) / math.sqrt(length * seq_count)
    conv_wide = lax.optimization_barrier(conv_out).astype(jnp.float32)
    grad_wide = lax.optimization_barrier(conv_grad).astype(jnp.float32)
    query_grad = (upstream.astype(jnp.float32) * conv_wide).astype(jnp.bfloat16)
    key_grad = (grad_wide * value_in.astype(jnp.float32)).astype(jnp.bfloat16)
    value_grad = (grad_wide * keys_in.astype(jnp.float32)).astype(jnp.bfloat16)
    return (query_grad, key_grad, value_grad, filter_grad.astype(jnp.float32))

def reference(queries, keys_in, value_in, upstream, filter_taps):
    seq_count, length, channels = queries.shape
    block_size = math.gcd(channels, 256)
    block_count = channels // block_size

    def split_blocks(array):
        return jnp.moveaxis(array.reshape(seq_count, length, block_count, block_size), 2, 0)

    def merge_blocks(array):
        return jnp.moveaxis(array, 0, 2).reshape(seq_count, length, channels)
    tap_blocks = jnp.moveaxis(filter_taps.reshape(length, block_count, block_size), 1, 0)
    results = lax.map(block_grads, (split_blocks(queries), split_blocks(keys_in), split_blocks(value_in), split_blocks(upstream), tap_blocks))
    filter_grad = jnp.moveaxis(results[3], 0, 1).reshape(length, channels)
    return (merge_blocks(results[0]), merge_blocks(results[1]), merge_blocks(results[2]), filter_grad)
```

```python
import functools
import math

import jax
import jax.numpy as jnp
import numpy as np
from jax import lax
from jax.experimental import pallas as pl
from jax.experimental.pallas import tpu as pltpu
from jax.sharding import PartitionSpec as P

BLOCK = 256
HALF = 64
LANES = 128
F32 = jnp.float32
BF16 = jnp.bfloat16
VMEM_LIMIT = 48 * 1024 * 1024


def dft_tables():
    freq = np.arange(BLOCK)[:, None] * 2 + 1
    time = np.arange(BLOCK)[None, :]
    angle = (freq * time % (4 * BLOCK)) * (2.0 * math.pi / (4 * BLOCK))
    forward = np.concatenate((np.cos(angle), -np.sin(angle)), axis=0).astype(np.float32)
    upper = forward.astype(jnp.bfloat16)
    lower = (forward - upper.astype(np.float32)).astype(jnp.bfloat16)
    inverse = (forward.T / BLOCK).astype(jnp.bfloat16)
    return upper, lower, inverse


def low_lanes(shape):
    return lax.broadcasted_iota(jnp.int32, shape, len(shape) - 1) < HALF


def swap_halves(first, second):
    mask = low_lanes(first.shape)
    return (
        jnp.where(mask, first, pltpu.roll(second, HALF, 1)),
        jnp.where(mask, pltpu.roll(first, HALF, 1), second),
    )


def row_signs(shape):
    row = lax.broadcasted_iota(jnp.int32, shape, 0)
    return (1 - 2 * (row % 2)).astype(F32)


def gate_kernel(q_ref, k_ref, v_ref, u_ref, out_ref):
    blocks = out_ref.shape[1]
    half_rows = out_ref.shape[3]
    for block in range(blocks):
        for pair in range(2):
            lanes = pl.ds((block * 2 + pair) * LANES, LANES)
            kv = k_ref[:, lanes].astype(F32) * v_ref[:, lanes].astype(F32)
            gg = u_ref[:, lanes].astype(F32) * q_ref[:, lanes].astype(F32)
            for signal, value in enumerate((kv, gg)):
                even, odd = swap_halves(value[:half_rows], value[half_rows:])
                out_ref[2 * pair, block, signal] = even.astype(BF16)
                out_ref[2 * pair + 1, block, signal] = odd.astype(BF16)


def filter_kernel(place_ref, taps_ref, upper_ref, lower_ref, out_ref):
    blocks = out_ref.shape[0]
    odd = place_ref[0] % 2
    signs = row_signs((BLOCK, LANES))
    mask = low_lanes((BLOCK, LANES))
    before = None
    for block in range(blocks):
        taps = taps_ref[pl.ds(block * BLOCK, BLOCK), :]
        turned = pltpu.roll(taps, HALF, 1)
        taps = jnp.where(jnp.logical_xor(mask, odd == 1), taps, turned)
        high = taps.astype(BF16)
        low = (taps - high.astype(F32)).astype(BF16)
        spec = jnp.dot(upper_ref[...], high, preferred_element_type=F32)
        spec = spec + jnp.dot(upper_ref[...], low, preferred_element_type=F32)
        spec = spec + jnp.dot(lower_ref[...], high, preferred_element_type=F32)
        real, imag = spec[:BLOCK], spec[BLOCK:]
        if before is None:
            out_ref[block, :BLOCK] = real
            out_ref[block, BLOCK:] = imag
        else:
            out_ref[block, :BLOCK] = real - signs * before[1]
            out_ref[block, BLOCK:] = imag + signs * before[0]
        before = (real, imag)


def conv_kernel(
    arrived_ref, filt_ref, forward_ref, inverse_ref, out_ref, grad_ref, sig_ref, spec_ref, prod_ref
):
    blocks = filt_ref.shape[0]
    slots = arrived_ref.shape[1]
    half_rows = arrived_ref.shape[3]
    per_block = slots // blocks
    for signal in range(2):
        for slot in range(slots):
            for pair in range(2):
                lanes = pl.ds(pair * LANES, LANES)
                first, second = swap_halves(
                    arrived_ref[2 * pair, slot, signal].astype(F32),
                    arrived_ref[2 * pair + 1, slot, signal].astype(F32),
                )
                at = (slot % per_block) * 2 * half_rows
                sig_ref[signal, slot // per_block, pl.ds(at, half_rows), lanes] = first.astype(BF16)
                sig_ref[signal, slot // per_block, pl.ds(at + half_rows, half_rows), lanes] = (
                    second.astype(BF16)
                )
    for signal in range(2):
        for block in range(blocks):
            spec_ref[signal, block] = jnp.dot(
                forward_ref[...], sig_ref[signal, block], preferred_element_type=F32
            )

    rows_at_once = 16
    signs = row_signs((rows_at_once, LANES))

    def tile(step, carry):
        row = pl.multiple_of((step // 2) * rows_at_once, rows_at_once)
        real_rows = pl.ds(row, rows_at_once)
        imag_rows = pl.ds(BLOCK + row, rows_at_once)
        lanes = pl.ds(pl.multiple_of((step % 2) * LANES, LANES), LANES)
        filt = [(filt_ref[b, real_rows, :], filt_ref[b, imag_rows, :]) for b in range(blocks)]
        value = [
            (spec_ref[0, b, real_rows, lanes], spec_ref[0, b, imag_rows, lanes]) for b in range(blocks)
        ]
        grad = [
            (spec_ref[1, b, real_rows, lanes], spec_ref[1, b, imag_rows, lanes]) for b in range(blocks)
        ]
        window = []
        for b in range(blocks):
            if b + 1 < blocks:
                window.append(
                    (grad[b][0] + signs * grad[b + 1][1], grad[b][1] - signs * grad[b + 1][0])
                )
            else:
                window.append(grad[b])

        def store(kind, block, real, imag):
            prod_ref[kind, block, real_rows, lanes] = real.astype(BF16)
            prod_ref[kind, block, imag_rows, lanes] = imag.astype(BF16)

        def total(terms):
            out = None
            for term in terms:
                out = term if out is None else out + term
            return out

        for b in range(blocks):
            pairs = [(filt[j], value[b - j]) for j in range(b + 1)]
            store(
                0,
                b,
                total([h[0] * x[0] - h[1] * x[1] for h, x in pairs]),
                total([h[0] * x[1] + h[1] * x[0] for h, x in pairs]),
            )
        for b in range(blocks):
            pairs = [(filt[j], grad[b + j]) for j in range(blocks - b)]
            store(
                1,
                b,
                total([h[0] * x[0] + h[1] * x[1] for h, x in pairs]),
                total([h[0] * x[1] - h[1] * x[0] for h, x in pairs]),
            )
        for b in range(blocks):
            pairs = [(value[j], window[b + j]) for j in range(blocks - b)]
            store(
                2,
                b,
                total([h[0] * x[0] + h[1] * x[1] for h, x in pairs]),
                total([h[0] * x[1] - h[1] * x[0] for h, x in pairs]),
            )
        return carry

    lax.fori_loop(0, BLOCK // rows_at_once * 2, tile, 0)

    mask = low_lanes((BLOCK, LANES))
    folded = []
    for block in range(blocks):
        cross = jnp.dot(inverse_ref[...], prod_ref[2, block], preferred_element_type=F32)
        cross = cross[:, :LANES] + cross[:, LANES:]
        folded.append(cross + pltpu.roll(cross, HALF, 1))
        if block >= blocks // 2:
            at = block - blocks // 2
            grad_ref[pl.ds(at * BLOCK, BLOCK), :] = jnp.where(
                mask, folded[at], folded[block]
            ).astype(BF16)
    for signal in range(2):
        for block in range(blocks):
            result = jnp.dot(inverse_ref[...], prod_ref[signal, block], preferred_element_type=F32)
            for part in range(per_block):
                for pair in range(2):
                    at = part * 2 * half_rows
                    lanes = slice(pair * LANES, (pair + 1) * LANES)
                    even, odd = swap_halves(
                        result[at : at + half_rows, lanes],
                        result[at + half_rows : at + 2 * half_rows, lanes],
                    )
                    slot = block * per_block + part
                    out_ref[2 * pair, slot, signal] = even.astype(BF16)
                    out_ref[2 * pair + 1, slot, signal] = odd.astype(BF16)


def final_kernel(ret_ref, k_ref, v_ref, u_ref, dq_ref, dk_ref, dv_ref):
    blocks = ret_ref.shape[1]
    half_rows = ret_ref.shape[3]
    for block in range(blocks):
        for pair in range(2):
            lanes = pl.ds((block * 2 + pair) * LANES, LANES)
            conv = swap_halves(
                ret_ref[2 * pair, block, 0].astype(F32), ret_ref[2 * pair + 1, block, 0].astype(F32)
            )
            back = swap_halves(
                ret_ref[2 * pair, block, 1].astype(F32), ret_ref[2 * pair + 1, block, 1].astype(F32)
            )
            for part in range(2):
                rows = pl.ds(part * half_rows, half_rows)
                dq_ref[rows, lanes] = (u_ref[rows, lanes].astype(F32) * conv[part]).astype(BF16)
                dk_ref[rows, lanes] = (back[part] * v_ref[rows, lanes].astype(F32)).astype(BF16)
                dv_ref[rows, lanes] = (back[part] * k_ref[rows, lanes].astype(F32)).astype(BF16)


def spread_kernel(gathered_ref, out_ref, *, scale):
    rows = gathered_ref.shape[1]
    for pair in range(2):
        lanes = pl.ds(pair * LANES, LANES)
        first, second = swap_halves(
            gathered_ref[2 * pair].astype(F32) * scale, gathered_ref[2 * pair + 1].astype(F32) * scale
        )
        out_ref[pl.ds(0, rows), lanes] = first
        out_ref[pl.ds(rows, rows), lanes] = second


def local(queries, keys_in, value_in, upstream, filter_taps, *, ctx_count, seq_count):
    tokens, channels = queries.shape[1], queries.shape[2]
    length = filter_taps.shape[0]
    blocks = length // BLOCK
    y_count = 4
    z_count = seq_count // y_count
    half_rows = tokens // 2
    q2, k2, v2, u2 = (a.reshape(tokens, channels) for a in (queries, keys_in, value_in, upstream))
    params = pltpu.CompilerParams(vmem_limit_bytes=VMEM_LIMIT)
    upper, lower, inverse = (jnp.asarray(t) for t in dft_tables())
    groups = [
        [(z * y_count + y) * ctx_count + c for y in range(y_count) for c in range(ctx_count)]
        for z in range(z_count)
    ]

    steps = 4
    part = ctx_count // steps
    gate_in = pl.BlockSpec((tokens, part * BLOCK), lambda i: (0, i))
    packed_spec = pl.BlockSpec((y_count, part, 2, half_rows, LANES), lambda i: (0, i, 0, 0, 0))
    packed_shape = jax.ShapeDtypeStruct((y_count, ctx_count, 2, half_rows, LANES), BF16)
    packed = pl.pallas_call(
        gate_kernel,
        grid=(steps,),
        in_specs=[gate_in] * 4,
        out_specs=packed_spec,
        out_shape=packed_shape,
        compiler_params=params,
        name="gate",
    )(q2, k2, v2, u2)

    def exchange(array):
        flat = array.reshape((y_count * ctx_count,) + array.shape[2:])
        moved = lax.all_to_all(flat, ("seq", "ctx"), 0, 0, tiled=True, axis_index_groups=groups)
        return moved.reshape(array.shape)

    arrived = exchange(packed)

    place = lax.rem(lax.axis_index("seq"), y_count).astype(jnp.int32).reshape(1)
    filt = pl.pallas_call(
        filter_kernel,
        grid_spec=pltpu.PrefetchScalarGridSpec(
            num_scalar_prefetch=1,
            grid=(1,),
            in_specs=[
                pl.BlockSpec((length, LANES), lambda i, place: (0, place[0] // 2)),
                pl.BlockSpec((2 * BLOCK, BLOCK), lambda i, place: (0, 0)),
                pl.BlockSpec((2 * BLOCK, BLOCK), lambda i, place: (0, 0)),
            ],
            out_specs=pl.BlockSpec((blocks, 2 * BLOCK, LANES), lambda i, place: (0, 0, 0)),
        ),
        out_shape=jax.ShapeDtypeStruct((blocks, 2 * BLOCK, LANES), F32),
        compiler_params=params,
        name="filter_spectra",
    )(place, filter_taps, upper, lower)

    whole = pl.BlockSpec(memory_space=pltpu.VMEM)
    outgoing, part_grad = pl.pallas_call(
        conv_kernel,
        in_specs=[whole] * 4,
        out_specs=[whole] * 2,
        out_shape=[packed_shape, jax.ShapeDtypeStruct((length // 2, LANES), BF16)],
        scratch_shapes=[
            pltpu.VMEM((2, blocks, BLOCK, 2 * LANES), BF16),
            pltpu.VMEM((2, blocks, 2 * BLOCK, 2 * LANES), F32),
            pltpu.VMEM((3, blocks, 2 * BLOCK, 2 * LANES), BF16),
        ],
        compiler_params=params,
        name="convolve",
    )(arrived, filt, upper, inverse)

    swapped = lax.ppermute(
        part_grad, "seq", [(s, (s + y_count) % seq_count) for s in range(seq_count)]
    )
    returned = exchange(outgoing)
    summed = (part_grad.astype(F32) + swapped.astype(F32)).astype(BF16)
    gathered = lax.all_gather(
        summed,
        "seq",
        axis=0,
        tiled=False,
        axis_index_groups=[[z * y_count + y for y in range(y_count)] for z in range(z_count)],
    )

    shape = jax.ShapeDtypeStruct((tokens, channels), BF16)
    query_grad, key_grad, value_grad = pl.pallas_call(
        final_kernel,
        grid=(steps,),
        in_specs=[packed_spec] + [gate_in] * 3,
        out_specs=[gate_in] * 3,
        out_shape=[shape] * 3,
        compiler_params=params,
        name="products",
    )(returned, k2, v2, u2)

    filter_grad = pl.pallas_call(
        functools.partial(spread_kernel, scale=1.0 / math.sqrt(length * seq_count)),
        in_specs=[whole],
        out_specs=whole,
        out_shape=jax.ShapeDtypeStruct((length, 2 * LANES), F32),
        compiler_params=params,
        name="spread",
    )(gathered)
    return (
        query_grad.reshape(queries.shape),
        key_grad.reshape(queries.shape),
        value_grad.reshape(queries.shape),
        filter_grad,
    )


def solution(mesh):
    return jax.shard_map(
        functools.partial(local, ctx_count=mesh.shape["ctx"], seq_count=mesh.shape["seq"]),
        mesh=mesh,
        in_specs=(
            P("seq", "ctx", None),
            P("seq", "ctx", None),
            P("seq", "ctx", None),
            P("seq", "ctx", None),
            P(None, "ctx"),
        ),
        out_specs=(
            P("seq", "ctx", None),
            P("seq", "ctx", None),
            P("seq", "ctx", None),
            P(None, "ctx"),
        ),
        check_vma=False,
    )
```

```python
import functools
import math
import random

import jax
import jax.numpy as jnp
import numpy as np
from jax import lax
from jax.experimental import pallas as pl
from jax.experimental.pallas import tpu as pltpu
from jax.sharding import PartitionSpec as P

BLOCK = 256
HALF = 64
LANES = 128
F32 = jnp.float32
BF16 = jnp.bfloat16
TILE = 16
CHUNKS = 4
VMEM_LIMIT = 30 * 1024 * 1024
SMALL_LIMIT = 12 * 1024 * 1024


def member_order(count):
    order = list(range(count))
    random.Random(58).shuffle(order)
    return order


def dft_tables():
    freq = np.arange(BLOCK)[:, None] * 2 + 1
    time = np.arange(BLOCK)[None, :]
    angle = (freq * time % (4 * BLOCK)) * (2.0 * math.pi / (4 * BLOCK))
    forward = np.concatenate((np.cos(angle), -np.sin(angle)), axis=0).astype(np.float32)
    upper = forward.astype(jnp.bfloat16)
    lower = (forward - upper.astype(np.float32)).astype(jnp.bfloat16)
    inverse = (forward.T / BLOCK).astype(jnp.bfloat16)
    return upper, lower, inverse


def low_lanes(shape):
    return lax.broadcasted_iota(jnp.int32, shape, len(shape) - 1) < HALF


def swap_halves(first, second):
    mask = low_lanes(first.shape)
    return (
        jnp.where(mask, first, pltpu.roll(second, HALF, 1)),
        jnp.where(mask, pltpu.roll(first, HALF, 1), second),
    )


def row_signs(shape):
    row = lax.broadcasted_iota(jnp.int32, shape, 0)
    return (1 - 2 * (row % 2)).astype(F32)


def gate_kernel(
    q_hbm, k_hbm, v_hbm, u_hbm, out_hbm,
    q_ref, k_ref, v_ref, u_ref, out_ref, in_sem, out_sem, *, slots
):
    half_rows = out_ref.shape[3]
    width = q_ref.shape[1] // CHUNKS
    count = width // BLOCK
    sources = ((q_hbm, q_ref), (k_hbm, k_ref), (v_hbm, v_ref), (u_hbm, u_ref))
    loads = [load_chunk(sources, in_sem, chunk, width) for chunk in range(CHUNKS)]
    for row in loads:
        for copy in row:
            copy.start()
    stores = []
    for chunk in range(CHUNKS):
        for copy in loads[chunk]:
            copy.wait()

        for block in range(chunk * count, (chunk + 1) * count):
            for pair in range(2):
                lanes = pl.ds((block * 2 + pair) * LANES, LANES)
                kv = k_ref[:, lanes].astype(F32) * v_ref[:, lanes].astype(F32)
                gg = u_ref[:, lanes].astype(F32) * q_ref[:, lanes].astype(F32)
                for signal, value in enumerate((kv, gg)):
                    parts = swap_halves(value[:half_rows], value[half_rows:])
                    for odd in range(2):
                        out_ref[2 * pair + odd, block, signal] = parts[odd].astype(BF16)
            for y, row in enumerate(slots):
                copy = pltpu.make_async_copy(
                    out_ref.at[y, block], out_hbm.at[row[block]], out_sem.at[row[block]]
                )
                copy.start()
                stores.append(copy)
    for copy in stores:
        copy.wait()


def load_chunk(pairs, sem, chunk, width):
    lanes = pl.ds(chunk * width, width)
    return [
        pltpu.make_async_copy(source.at[:, lanes], target.at[:, lanes], sem.at[which, chunk])
        for which, (source, target) in enumerate(pairs)
    ]


def filter_kernel(place_ref, taps_ref, upper_ref, lower_ref, out_ref):
    blocks = out_ref.shape[1]
    odd = place_ref[0] % 2
    signs = row_signs((BLOCK, LANES))
    mask = low_lanes((BLOCK, LANES))
    before = None
    for block in range(blocks):
        taps = taps_ref[pl.ds(block * BLOCK, BLOCK), :]
        turned = pltpu.roll(taps, HALF, 1)
        taps = jnp.where(jnp.logical_xor(mask, odd == 1), taps, turned)
        high = taps.astype(BF16)
        low = (taps - high.astype(F32)).astype(BF16)
        spec = jnp.dot(upper_ref[...], high, preferred_element_type=F32)
        spec = spec + jnp.dot(upper_ref[...], low, preferred_element_type=F32)
        spec = spec + jnp.dot(lower_ref[...], high, preferred_element_type=F32)
        real, imag = spec[:BLOCK], spec[BLOCK:]
        after = (real, imag)
        if before is not None:
            real, imag = real - signs * before[1], imag + signs * before[0]
        out_ref[0, block] = real
        out_ref[1, block] = imag
        before = after


def spectrum(arrived_ref, forward_ref, sig_ref, spec_ref, slots, signal):
    half_rows = arrived_ref.shape[2]
    per_block = BLOCK // (2 * half_rows)
    for block in range(spec_ref.shape[0]):
        for part in range(per_block):
            for pair in range(2):
                lanes = pl.ds(pair * LANES, LANES)
                first, second = swap_halves(
                    *(
                        arrived_ref[slots[2 * pair + odd][block * per_block + part], signal].astype(F32)
                        for odd in range(2)
                    )
                )
                at = part * 2 * half_rows
                sig_ref[block, pl.ds(at, half_rows), lanes] = first.astype(BF16)
                sig_ref[block, pl.ds(at + half_rows, half_rows), lanes] = second.astype(BF16)
        spec_ref[block] = jnp.dot(forward_ref[...], sig_ref[block], preferred_element_type=F32)


def total(terms):
    out = None
    for term in terms:
        out = term if out is None else out + term
    return out


def side(real, imag):
    return real, imag - real, real + imag


def multiply(pairs):
    first, second, third = (total([h[i] * x[i] for h, x in pairs]) for i in range(3))
    return first - third, first + second


def multiply_conj(pairs):
    first, second, third = (total([h[i] * x[i] for h, x in pairs]) for i in range(3))
    return first + third, first + second


def tile_slices(step):
    row = pl.multiple_of((step // 2) * TILE, TILE)
    lanes = pl.ds(pl.multiple_of((step % 2) * LANES, LANES), LANES)
    return pl.ds(row, TILE), pl.ds(BLOCK + row, TILE), lanes


def read_tiles(spec_ref, where):
    real_rows, imag_rows, lanes = where
    return [
        (spec_ref[b, real_rows, lanes], spec_ref[b, imag_rows, lanes]) for b in range(spec_ref.shape[0])
    ]


def write_tile(prod_ref, where, block, value):
    real_rows, imag_rows, lanes = where
    prod_ref[block, real_rows, lanes] = value[0].astype(BF16)
    prod_ref[block, imag_rows, lanes] = value[1].astype(BF16)


def cross_kernel(
    arrived_ref, forward_ref, inverse_ref, after_ref, terms_ref,
    sig_ref, value_ref, grad_ref, prod_ref, *, slots
):
    blocks = value_ref.shape[0]
    spectrum(arrived_ref, forward_ref, sig_ref, value_ref, slots, 0)
    spectrum(arrived_ref, forward_ref, sig_ref, grad_ref, slots, 1)
    signs = row_signs((TILE, LANES))

    def tile(step, carry):
        where = tile_slices(step)
        value, grad = read_tiles(value_ref, where), read_tiles(grad_ref, where)
        window = [
            (grad[b][0] + signs * grad[b + 1][1], grad[b][1] - signs * grad[b + 1][0])
            for b in range(blocks - 1)
        ] + [grad[-1]]
        left = [(real - imag, real, imag) for real, imag in value]
        right = [side(*x) for x in window]
        for b in range(blocks):
            write_tile(
                prod_ref, where, b, multiply_conj([(left[j], right[b + j]) for j in range(blocks - b)])
            )
        return carry

    lax.fori_loop(0, BLOCK // TILE * 2, tile, 0)

    mask = low_lanes((BLOCK, LANES))
    folded = []
    for block in range(blocks):
        cross = jnp.dot(inverse_ref[...], prod_ref[block], preferred_element_type=F32)
        cross = cross[:, :LANES] + cross[:, LANES:]
        folded.append(cross + pltpu.roll(cross, HALF, 1))
        if block >= blocks // 2:
            at = block - blocks // 2
            terms_ref[pl.ds(at * BLOCK, BLOCK), :] = jnp.where(
                mask, folded[at], folded[block]
            ).astype(BF16)


def conv_kernel(
    arrived_ref, filt_hbm, forward_ref, inverse_ref, after_ref, out_hbm,
    filt_ref, sig_ref, value_ref, grad_ref, conv_ref, back_ref, out_ref, filt_sem, out_sem, *, slots
):
    load = pltpu.make_async_copy(filt_hbm, filt_ref, filt_sem)
    load.start()
    blocks = value_ref.shape[0]
    half_rows = out_ref.shape[2]
    per_block = BLOCK // (2 * half_rows)
    spectrum(arrived_ref, forward_ref, sig_ref, value_ref, slots, 0)
    spectrum(arrived_ref, forward_ref, sig_ref, grad_ref, slots, 1)
    load.wait()

    def tile(step, carry):
        where = tile_slices(step)
        rows = where[0]
        filt = [(filt_ref[0, b, rows, :], filt_ref[1, b, rows, :]) for b in range(blocks)]
        left = [(real + imag, real, imag) for real, imag in filt]
        right = [side(*x) for x in read_tiles(value_ref, where)]
        for b in range(blocks):
            write_tile(conv_ref, where, b, multiply([(left[j], right[b - j]) for j in range(b + 1)]))
        left = [(real - imag, real, imag) for real, imag in filt]
        right = [side(*x) for x in read_tiles(grad_ref, where)]
        for b in range(blocks):
            write_tile(
                back_ref, where, b, multiply_conj([(left[j], right[b + j]) for j in range(blocks - b)])
            )
        return carry

    lax.fori_loop(0, BLOCK // TILE * 2, tile, 0)

    stores = []
    for block in range(blocks):
        for signal, prod_ref in enumerate((conv_ref, back_ref)):
            result = jnp.dot(inverse_ref[...], prod_ref[block], preferred_element_type=F32)
            for part in range(per_block):
                at = part * 2 * half_rows
                for pair in range(2):
                    lanes = slice(pair * LANES, (pair + 1) * LANES)
                    parts = swap_halves(
                        result[at : at + half_rows, lanes],
                        result[at + half_rows : at + 2 * half_rows, lanes],
                    )
                    for odd in range(2):
                        place = slots[2 * pair + odd][block * per_block + part]
                        out_ref[place, signal] = parts[odd].astype(BF16)
        for part in range(per_block):
            for row in slots:
                place = row[block * per_block + part]
                copy = pltpu.make_async_copy(out_ref.at[place], out_hbm.at[place], out_sem.at[place])
                copy.start()
                stores.append(copy)
    for copy in stores:
        copy.wait()


def final_kernel(
    ret_ref, k_ref, v_ref, u_ref, dq_hbm, dk_hbm, dv_hbm, dq_ref, dk_ref, dv_ref, out_sem, *, slots
):
    half_rows = ret_ref.shape[2]
    width = k_ref.shape[1] // CHUNKS
    count = width // BLOCK
    targets = ((dq_ref, dq_hbm), (dk_ref, dk_hbm), (dv_ref, dv_hbm))
    stores = [load_chunk(targets, out_sem, chunk, width) for chunk in range(CHUNKS)]
    for chunk in range(CHUNKS):
        for block in range(chunk * count, (chunk + 1) * count):
            for pair in range(2):
                lanes = pl.ds((block * 2 + pair) * LANES, LANES)
                conv, back = (
                    swap_halves(
                        *(ret_ref[slots[2 * pair + odd][block], signal].astype(F32) for odd in range(2))
                    )
                    for signal in range(2)
                )
                for part in range(2):
                    rows = pl.ds(part * half_rows, half_rows)
                    dq_ref[rows, lanes] = (u_ref[rows, lanes].astype(F32) * conv[part]).astype(BF16)
                    dk_ref[rows, lanes] = (back[part] * v_ref[rows, lanes].astype(F32)).astype(BF16)
                    dv_ref[rows, lanes] = (back[part] * k_ref[rows, lanes].astype(F32)).astype(BF16)
        for copy in stores[chunk]:
            copy.start()
    for row in stores:
        for copy in row:
            copy.wait()


def spread_kernel(place_ref, own_ref, up_ref, down_ref, far_ref, out_ref, held_ref, *, scale):
    count = held_ref.shape[0]
    rows = held_ref.shape[1]
    place = place_ref[0]
    for ref, shift in ((own_ref, 0), (up_ref, 1), (down_ref, 3), (far_ref, 2)):
        held_ref[lax.rem(place + count - shift, count)] = ref[...]
    for pair in range(2):
        lanes = pl.ds(pair * LANES, LANES)
        first, second = swap_halves(
            held_ref[2 * pair].astype(F32) * scale, held_ref[2 * pair + 1].astype(F32) * scale
        )
        out_ref[pl.ds(0, rows), lanes] = first
        out_ref[pl.ds(rows, rows), lanes] = second


def local(queries, keys_in, value_in, upstream, filter_taps, *, ctx_count, seq_count):
    tokens, channels = queries.shape[1], queries.shape[2]
    length = filter_taps.shape[0]
    blocks = length // BLOCK
    y_count = 4
    z_count = seq_count // y_count
    half_rows = tokens // 2
    tokens_in = [a.reshape(tokens, channels) for a in (queries, keys_in, value_in, upstream)]
    params = pltpu.CompilerParams(vmem_limit_bytes=VMEM_LIMIT)
    upper, lower, inverse = (jnp.asarray(t) for t in dft_tables())
    members = y_count * ctx_count
    order = member_order(members)
    groups = [[z * members + m for m in order] for z in range(z_count)]
    place_of = [[order.index(y * ctx_count + c) for c in range(ctx_count)] for y in range(y_count)]
    hbm = pl.BlockSpec(memory_space=pltpu.HBM)
    whole = pl.BlockSpec(memory_space=pltpu.VMEM)
    scalars = pl.BlockSpec(memory_space=pltpu.SMEM)
    token_tile = pltpu.VMEM((tokens, channels), BF16)
    packed_shape = (members, 2, half_rows, LANES)

    packed = pl.pallas_call(
        functools.partial(gate_kernel, slots=place_of),
        in_specs=[hbm] * 4,
        out_specs=hbm,
        out_shape=pltpu.HBM(packed_shape, BF16),
        scratch_shapes=[token_tile] * 4
        + [
            pltpu.VMEM((y_count, ctx_count) + packed_shape[1:], BF16),
            pltpu.SemaphoreType.DMA((4, CHUNKS)),
            pltpu.SemaphoreType.DMA((members,)),
        ],
        compiler_params=params,
        name="gate",
    )(*(pltpu.with_memory_space_constraint(a, pltpu.HBM) for a in tokens_in))

    def exchange(array):
        return lax.all_to_all(array, ("seq", "ctx"), 0, 0, tiled=True, axis_index_groups=groups)

    arrived = exchange(packed)

    place = lax.rem(lax.axis_index("seq"), y_count).astype(jnp.int32).reshape(1)
    filt = pl.pallas_call(
        filter_kernel,
        grid_spec=pltpu.PrefetchScalarGridSpec(
            num_scalar_prefetch=1,
            grid=(1,),
            in_specs=[
                pl.BlockSpec((length, LANES), lambda i, place: (0, place[0] // 2)),
                pl.BlockSpec((2 * BLOCK, BLOCK), lambda i, place: (0, 0)),
                pl.BlockSpec((2 * BLOCK, BLOCK), lambda i, place: (0, 0)),
            ],
            out_specs=pl.BlockSpec((2, blocks, BLOCK, LANES), lambda i, place: (0, 0, 0, 0)),
        ),
        out_shape=pltpu.HBM((2, blocks, BLOCK, LANES), F32),
        compiler_params=params,
        name="filter_spectra",
    )(place, filter_taps, upper, lower)
    filt = pltpu.with_memory_space_constraint(filt, pltpu.HBM)

    signal_tile = pltpu.VMEM((blocks, BLOCK, 2 * LANES), BF16)
    spectrum_tile = pltpu.VMEM((blocks, 2 * BLOCK, 2 * LANES), F32)
    product_tile = pltpu.VMEM((blocks, 2 * BLOCK, 2 * LANES), BF16)
    part_grad = pl.pallas_call(
        functools.partial(cross_kernel, slots=place_of),
        in_specs=[whole] * 3 + [hbm],
        out_specs=whole,
        out_shape=jax.ShapeDtypeStruct((length // 2, LANES), BF16),
        scratch_shapes=[signal_tile, spectrum_tile, spectrum_tile, product_tile],
        compiler_params=params,
        name="filter_terms",
    )(arrived, upper, inverse, filt)

    outgoing = pl.pallas_call(
        functools.partial(conv_kernel, slots=place_of),
        in_specs=[whole, hbm, whole, whole, pl.BlockSpec(memory_space=pl.ANY)],
        out_specs=hbm,
        out_shape=pltpu.HBM(packed_shape, BF16),
        scratch_shapes=[
            pltpu.VMEM(filt.shape, F32),
            signal_tile,
            spectrum_tile,
            spectrum_tile,
            product_tile,
            product_tile,
            pltpu.VMEM(packed_shape, BF16),
            pltpu.SemaphoreType.DMA,
            pltpu.SemaphoreType.DMA((members,)),
        ],
        compiler_params=params,
        name="convolve",
    )(arrived, filt, upper, inverse, part_grad)
    swapped = lax.ppermute(
        part_grad, "seq", [(s, (s + y_count) % seq_count) for s in range(seq_count)]
    )
    summed = (part_grad.astype(F32) + swapped.astype(F32)).astype(BF16)
    outgoing, summed = lax.optimization_barrier((outgoing, summed))
    others = [
        lax.ppermute(
            summed,
            "seq",
            [(s, s // y_count * y_count + (s + shift) % y_count) for s in range(seq_count)],
        )
        for shift in (1, 3, 2)
    ]
    returned = exchange(outgoing)
    query_grad, key_grad, value_grad = pl.pallas_call(
        functools.partial(final_kernel, slots=place_of),
        in_specs=[whole] * 4,
        out_specs=[hbm] * 3,
        out_shape=[pltpu.HBM((tokens, channels), BF16)] * 3,
        scratch_shapes=[token_tile] * 3 + [pltpu.SemaphoreType.DMA((3, CHUNKS))],
        compiler_params=pltpu.CompilerParams(vmem_limit_bytes=SMALL_LIMIT),
        name="products",
    )(returned, *tokens_in[1:])
    query_grad, summed, *others = lax.optimization_barrier((query_grad, summed, *others))
    filter_grad = pl.pallas_call(
        functools.partial(spread_kernel, scale=1.0 / math.sqrt(length * seq_count)),
        in_specs=[scalars] + [whole] * 4,
        out_specs=whole,
        out_shape=jax.ShapeDtypeStruct((length, 2 * LANES), F32),
        scratch_shapes=[pltpu.VMEM((y_count, length // 2, LANES), BF16)],
        compiler_params=params,
        name="spread",
    )(place, summed, *others)

    return (
        query_grad.reshape(queries.shape),
        key_grad.reshape(queries.shape),
        value_grad.reshape(queries.shape),
        filter_grad,
    )


def solution(mesh):
    return jax.shard_map(
        functools.partial(local, ctx_count=mesh.shape["ctx"], seq_count=mesh.shape["seq"]),
        mesh=mesh,
        in_specs=(
            P("seq", "ctx", None),
            P("seq", "ctx", None),
            P("seq", "ctx", None),
            P("seq", "ctx", None),
            P(None, "ctx"),
        ),
        out_specs=(
            P("seq", "ctx", None),
            P("seq", "ctx", None),
            P("seq", "ctx", None),
            P(None, "ctx"),
        ),
        check_vma=False,
    )
```

```python
import functools
import math
import random

import jax
import jax.numpy as jnp
import numpy as np
from jax import lax
from jax.experimental import pallas as pl
from jax.experimental.pallas import tpu as pltpu
from jax.sharding import PartitionSpec as P

BLOCK = 256
HALF = 64
LANES = 128
F32 = jnp.float32
BF16 = jnp.bfloat16
TILE = 16
CHUNKS = 4
VMEM_LIMIT = 24 * 1024 * 1024
SMALL_LIMIT = 12 * 1024 * 1024


def member_order(count):
    order = list(range(count))
    random.Random(58).shuffle(order)
    return order


def dft_tables():
    freq = np.arange(BLOCK)[:, None] * 2 + 1
    time = np.arange(BLOCK)[None, :]
    angle = (freq * time % (4 * BLOCK)) * (2.0 * math.pi / (4 * BLOCK))
    forward = np.concatenate((np.cos(angle), -np.sin(angle)), axis=0).astype(np.float32)
    upper = forward.astype(jnp.bfloat16)
    lower = (forward - upper.astype(np.float32)).astype(jnp.bfloat16)
    inverse = (forward.T / BLOCK).astype(jnp.bfloat16)
    return upper, lower, inverse


def low_lanes(shape):
    return lax.broadcasted_iota(jnp.int32, shape, len(shape) - 1) < HALF


def swap_halves(first, second):
    mask = low_lanes(first.shape)
    return (
        jnp.where(mask, first, pltpu.roll(second, HALF, 1)),
        jnp.where(mask, pltpu.roll(first, HALF, 1), second),
    )


def row_signs(shape):
    row = lax.broadcasted_iota(jnp.int32, shape, 0)
    return (1 - 2 * (row % 2)).astype(F32)


def gate_kernel(
    q_hbm, k_hbm, v_hbm, u_hbm, out_hbm,
    q_ref, k_ref, v_ref, u_ref, out_ref, in_sem, out_sem, *, slots
):
    half_rows = out_ref.shape[3]
    width = q_ref.shape[1] // CHUNKS
    count = width // BLOCK
    sources = ((q_hbm, q_ref), (k_hbm, k_ref), (v_hbm, v_ref), (u_hbm, u_ref))
    loads = [load_chunk(sources, in_sem, chunk, width) for chunk in range(CHUNKS)]
    for row in loads:
        for copy in row:
            copy.start()
    stores = []
    for chunk in range(CHUNKS):
        for copy in loads[chunk]:
            copy.wait()

        for block in range(chunk * count, (chunk + 1) * count):
            for pair in range(2):
                lanes = pl.ds((block * 2 + pair) * LANES, LANES)
                kv = k_ref[:, lanes].astype(F32) * v_ref[:, lanes].astype(F32)
                gg = u_ref[:, lanes].astype(F32) * q_ref[:, lanes].astype(F32)
                for signal, value in enumerate((kv, gg)):
                    parts = swap_halves(value[:half_rows], value[half_rows:])
                    for odd in range(2):
                        out_ref[2 * pair + odd, block, signal] = parts[odd].astype(BF16)
            for y, row in enumerate(slots):
                copy = pltpu.make_async_copy(
                    out_ref.at[y, block], out_hbm.at[row[block]], out_sem.at[row[block]]
                )
                copy.start()
                stores.append(copy)
    for copy in stores:
        copy.wait()


def load_chunk(pairs, sem, chunk, width):
    lanes = pl.ds(chunk * width, width)
    return [
        pltpu.make_async_copy(source.at[:, lanes], target.at[:, lanes], sem.at[which, chunk])
        for which, (source, target) in enumerate(pairs)
    ]


def filter_kernel(place_ref, taps_ref, upper_ref, lower_ref, out_ref):
    blocks = out_ref.shape[1]
    odd = place_ref[0] % 2
    signs = row_signs((BLOCK, LANES))
    mask = low_lanes((BLOCK, LANES))
    before = None
    for block in range(blocks):
        taps = taps_ref[pl.ds(block * BLOCK, BLOCK), :]
        turned = pltpu.roll(taps, HALF, 1)
        taps = jnp.where(jnp.logical_xor(mask, odd == 1), taps, turned)
        high = taps.astype(BF16)
        low = (taps - high.astype(F32)).astype(BF16)
        spec = jnp.dot(upper_ref[...], high, preferred_element_type=F32)
        spec = spec + jnp.dot(upper_ref[...], low, preferred_element_type=F32)
        spec = spec + jnp.dot(lower_ref[...], high, preferred_element_type=F32)
        real, imag = spec[:BLOCK], spec[BLOCK:]
        after = (real, imag)
        if before is not None:
            real, imag = real - signs * before[1], imag + signs * before[0]
        out_ref[0, block] = real
        out_ref[1, block] = imag
        before = after


def spectrum(arrived_ref, forward_ref, sig_ref, spec_ref, slots, signal):
    half_rows = arrived_ref.shape[2]
    per_block = BLOCK // (2 * half_rows)
    for block in range(spec_ref.shape[0]):
        for part in range(per_block):
            for pair in range(2):
                lanes = pl.ds(pair * LANES, LANES)
                first, second = swap_halves(
                    *(
                        arrived_ref[slots[2 * pair + odd][block * per_block + part], signal].astype(F32)
                        for odd in range(2)
                    )
                )
                at = part * 2 * half_rows
                sig_ref[block, pl.ds(at, half_rows), lanes] = first.astype(BF16)
                sig_ref[block, pl.ds(at + half_rows, half_rows), lanes] = second.astype(BF16)
        spec_ref[block] = jnp.dot(forward_ref[...], sig_ref[block], preferred_element_type=F32)


def total(terms):
    out = None
    for term in terms:
        out = term if out is None else out + term
    return out


def side(real, imag):
    return real, imag - real, real + imag


def multiply(pairs):
    first, second, third = (total([h[i] * x[i] for h, x in pairs]) for i in range(3))
    return first - third, first + second


def multiply_conj(pairs):
    first, second, third = (total([h[i] * x[i] for h, x in pairs]) for i in range(3))
    return first + third, first + second


def tile_slices(step):
    row = pl.multiple_of((step // 2) * TILE, TILE)
    lanes = pl.ds(pl.multiple_of((step % 2) * LANES, LANES), LANES)
    return pl.ds(row, TILE), pl.ds(BLOCK + row, TILE), lanes


def read_tiles(spec_ref, where):
    real_rows, imag_rows, lanes = where
    return [
        (spec_ref[b, real_rows, lanes], spec_ref[b, imag_rows, lanes]) for b in range(spec_ref.shape[0])
    ]


def write_tile(prod_ref, where, block, value):
    real_rows, imag_rows, lanes = where
    prod_ref[block, real_rows, lanes] = value[0].astype(BF16)
    prod_ref[block, imag_rows, lanes] = value[1].astype(BF16)


def cross_kernel(
    arrived_ref, forward_ref, inverse_ref, filt_hbm, terms_ref, value_ref, grad_ref, filt_ref,
    sig_ref, prod_ref, filt_sem, *, slots
):
    blocks = value_ref.shape[0]
    loads = filter_loads(filt_hbm, filt_ref, filt_sem)
    spectrum(arrived_ref, forward_ref, sig_ref, value_ref, slots, 0)
    spectrum(arrived_ref, forward_ref, sig_ref, grad_ref, slots, 1)
    signs = row_signs((TILE, LANES))

    def tile(step, carry):
        where = tile_slices(step)
        value, grad = read_tiles(value_ref, where), read_tiles(grad_ref, where)
        window = [
            (grad[b][0] + signs * grad[b + 1][1], grad[b][1] - signs * grad[b + 1][0])
            for b in range(blocks - 1)
        ] + [grad[-1]]
        left = [(real - imag, real, imag) for real, imag in value]
        right = [side(*x) for x in window]
        for b in range(blocks):
            write_tile(
                prod_ref, where, b, multiply_conj([(left[j], right[b + j]) for j in range(blocks - b)])
            )
        return carry

    lax.fori_loop(0, BLOCK // TILE * 2, tile, 0)

    mask = low_lanes((BLOCK, LANES))
    folded = []
    for block in range(blocks):
        cross = jnp.dot(inverse_ref[...], prod_ref[block], preferred_element_type=F32)
        cross = cross[:, :LANES] + cross[:, LANES:]
        folded.append(cross + pltpu.roll(cross, HALF, 1))
        if block >= blocks // 2:
            at = block - blocks // 2
            terms_ref[pl.ds(at * BLOCK, BLOCK), :] = jnp.where(
                mask, folded[at], folded[block]
            ).astype(BF16)
    for copy in loads:
        copy.wait()


def filter_loads(filt_hbm, filt_ref, sem):
    copies = [
        pltpu.make_async_copy(filt_hbm.at[kind, block], filt_ref.at[kind, block], sem.at[kind, block])
        for block in range(filt_ref.shape[1])
        for kind in range(2)
    ]
    for copy in copies:
        copy.start()
    return copies


def invert_block(inverse_ref, prod_ref, out_ref, block, slots, signal):
    half_rows = out_ref.shape[2]
    per_block = BLOCK // (2 * half_rows)
    result = jnp.dot(inverse_ref[...], prod_ref[block], preferred_element_type=F32)
    places = []
    for part in range(per_block):
        at = part * 2 * half_rows
        for pair in range(2):
            lanes = slice(pair * LANES, (pair + 1) * LANES)
            parts = swap_halves(
                result[at : at + half_rows, lanes], result[at + half_rows : at + 2 * half_rows, lanes]
            )
            for odd in range(2):
                place = slots[2 * pair + odd][block * per_block + part]
                out_ref[place, signal] = parts[odd].astype(BF16)
                places.append(place)
    return places


def conv_kernel(
    value_ref, grad_ref, filt_ref, inverse_ref, out_hbm, conv_ref, back_ref, out_ref, out_sem, *, slots
):
    blocks = value_ref.shape[0]

    def tile(step, carry):
        where = tile_slices(step)
        rows = where[0]
        filt = [(filt_ref[0, b, rows, :], filt_ref[1, b, rows, :]) for b in range(blocks)]
        left = [(real + imag, real, imag) for real, imag in filt]
        right = [side(*x) for x in read_tiles(value_ref, where)]
        for b in range(blocks):
            write_tile(conv_ref, where, b, multiply([(left[j], right[b - j]) for j in range(b + 1)]))
        left = [(real - imag, real, imag) for real, imag in filt]
        right = [side(*x) for x in read_tiles(grad_ref, where)]
        for b in range(blocks):
            write_tile(
                back_ref, where, b, multiply_conj([(left[j], right[b + j]) for j in range(blocks - b)])
            )
        return carry

    lax.fori_loop(0, BLOCK // TILE * 2, tile, 0)
    stores = []
    for block in range(blocks):
        for signal, prod_ref in enumerate((conv_ref, back_ref)):
            places = invert_block(inverse_ref, prod_ref, out_ref, block, slots, signal)
        for place in places:
            copy = pltpu.make_async_copy(out_ref.at[place], out_hbm.at[place], out_sem.at[place])
            copy.start()
            stores.append(copy)
    for copy in stores:
        copy.wait()


def final_kernel(
    ret_ref, k_ref, v_ref, u_ref, dq_hbm, dk_hbm, dv_hbm, dq_ref, dk_ref, dv_ref, out_sem, *, slots
):
    half_rows = ret_ref.shape[2]
    width = k_ref.shape[1] // CHUNKS
    count = width // BLOCK
    targets = ((dq_ref, dq_hbm), (dk_ref, dk_hbm), (dv_ref, dv_hbm))
    stores = [load_chunk(targets, out_sem, chunk, width) for chunk in range(CHUNKS)]
    for chunk in range(CHUNKS):
        for block in range(chunk * count, (chunk + 1) * count):
            for pair in range(2):
                lanes = pl.ds((block * 2 + pair) * LANES, LANES)
                conv, back = (
                    swap_halves(
                        *(ret_ref[slots[2 * pair + odd][block], signal].astype(F32) for odd in range(2))
                    )
                    for signal in range(2)
                )
                for part in range(2):
                    rows = pl.ds(part * half_rows, half_rows)
                    dq_ref[rows, lanes] = (u_ref[rows, lanes].astype(F32) * conv[part]).astype(BF16)
                    dk_ref[rows, lanes] = (back[part] * v_ref[rows, lanes].astype(F32)).astype(BF16)
                    dv_ref[rows, lanes] = (back[part] * k_ref[rows, lanes].astype(F32)).astype(BF16)
        for copy in stores[chunk]:
            copy.start()
    for row in stores:
        for copy in row:
            copy.wait()


def spread_kernel(
    place_ref, own_ref, up_ref, down_ref, far_ref, after_ref,
    out_hbm, held_ref, out_ref, out_sem, *, scale
):
    count = held_ref.shape[0]
    rows = held_ref.shape[1]
    step = rows // CHUNKS
    place = place_ref[0]
    for ref, shift in ((own_ref, 0), (up_ref, 1), (down_ref, 3), (far_ref, 2)):
        held_ref[lax.rem(place + count - shift, count)] = ref[...]
    stores = []
    for chunk in range(CHUNKS):
        part = pl.ds(chunk * step, step)
        for pair in range(2):
            lanes = pl.ds(pair * LANES, LANES)
            values = swap_halves(
                held_ref[2 * pair, part].astype(F32) * scale,
                held_ref[2 * pair + 1, part].astype(F32) * scale,
            )
            for half in range(2):
                out_ref[pl.ds(half * rows + chunk * step, step), lanes] = values[half]
        for half in range(2):
            part = pl.ds(half * rows + chunk * step, step)
            copy = pltpu.make_async_copy(out_ref.at[part], out_hbm.at[part], out_sem.at[half, chunk])
            copy.start()
            stores.append(copy)
    for copy in stores:
        copy.wait()


def local(queries, keys_in, value_in, upstream, filter_taps, *, ctx_count, seq_count):
    tokens, channels = queries.shape[1], queries.shape[2]
    length = filter_taps.shape[0]
    blocks = length // BLOCK
    y_count = 4
    z_count = seq_count // y_count
    half_rows = tokens // 2
    tokens_in = [a.reshape(tokens, channels) for a in (queries, keys_in, value_in, upstream)]
    params = pltpu.CompilerParams(vmem_limit_bytes=VMEM_LIMIT)
    upper, lower, inverse = (jnp.asarray(t) for t in dft_tables())
    members = y_count * ctx_count
    order = member_order(members)
    groups = [[z * members + m for m in order] for z in range(z_count)]
    place_of = [[order.index(y * ctx_count + c) for c in range(ctx_count)] for y in range(y_count)]
    hbm = pl.BlockSpec(memory_space=pltpu.HBM)
    whole = pl.BlockSpec(memory_space=pltpu.VMEM)
    scalars = pl.BlockSpec(memory_space=pltpu.SMEM)
    token_tile = pltpu.VMEM((tokens, channels), BF16)
    packed_shape = (members, 2, half_rows, LANES)

    packed = pl.pallas_call(
        functools.partial(gate_kernel, slots=place_of),
        in_specs=[hbm] * 4,
        out_specs=hbm,
        out_shape=pltpu.HBM(packed_shape, BF16),
        scratch_shapes=[token_tile] * 4
        + [
            pltpu.VMEM((y_count, ctx_count) + packed_shape[1:], BF16),
            pltpu.SemaphoreType.DMA((4, CHUNKS)),
            pltpu.SemaphoreType.DMA((members,)),
        ],
        compiler_params=params,
        name="gate",
    )(*(pltpu.with_memory_space_constraint(a, pltpu.HBM) for a in tokens_in))

    def exchange(array):
        return lax.all_to_all(array, ("seq", "ctx"), 0, 0, tiled=True, axis_index_groups=groups)

    arrived = exchange(packed)

    place = lax.rem(lax.axis_index("seq"), y_count).astype(jnp.int32).reshape(1)
    filt = pl.pallas_call(
        filter_kernel,
        grid_spec=pltpu.PrefetchScalarGridSpec(
            num_scalar_prefetch=1,
            grid=(1,),
            in_specs=[
                pl.BlockSpec((length, LANES), lambda i, place: (0, place[0] // 2)),
                pl.BlockSpec((2 * BLOCK, BLOCK), lambda i, place: (0, 0)),
                pl.BlockSpec((2 * BLOCK, BLOCK), lambda i, place: (0, 0)),
            ],
            out_specs=pl.BlockSpec((2, blocks, BLOCK, LANES), lambda i, place: (0, 0, 0, 0)),
        ),
        out_shape=pltpu.HBM((2, blocks, BLOCK, LANES), F32),
        compiler_params=params,
        name="filter_spectra",
    )(place, filter_taps, upper, lower)
    filt = pltpu.with_memory_space_constraint(filt, pltpu.HBM)

    signal_tile = pltpu.VMEM((blocks, BLOCK, 2 * LANES), BF16)
    product_tile = pltpu.VMEM((blocks, 2 * BLOCK, 2 * LANES), BF16)
    spectrum_shape = jax.ShapeDtypeStruct((blocks, 2 * BLOCK, 2 * LANES), F32)
    part_grad, value_spec, grad_spec, filt = pl.pallas_call(
        functools.partial(cross_kernel, slots=place_of),
        in_specs=[whole] * 3 + [hbm],
        out_specs=[whole] * 4,
        out_shape=[
            jax.ShapeDtypeStruct((length // 2, LANES), BF16),
            spectrum_shape,
            spectrum_shape,
            jax.ShapeDtypeStruct(filt.shape, F32),
        ],
        scratch_shapes=[signal_tile, product_tile, pltpu.SemaphoreType.DMA((2, blocks))],
        compiler_params=params,
        name="filter_terms",
    )(arrived, upper, inverse, filt)
    outgoing = pl.pallas_call(
        functools.partial(conv_kernel, slots=place_of),
        in_specs=[whole] * 4,
        out_specs=hbm,
        out_shape=pltpu.HBM(packed_shape, BF16),
        scratch_shapes=[
            product_tile,
            product_tile,
            pltpu.VMEM(packed_shape, BF16),
            pltpu.SemaphoreType.DMA((members,)),
        ],
        compiler_params=params,
        name="convolve",
    )(value_spec, grad_spec, filt, inverse)
    swapped = lax.ppermute(
        part_grad, "seq", [(s, (s + y_count) % seq_count) for s in range(seq_count)]
    )
    summed = (part_grad.astype(F32) + swapped.astype(F32)).astype(BF16)
    outgoing, summed = lax.optimization_barrier((outgoing, summed))
    others = [
        lax.ppermute(
            summed,
            "seq",
            [(s, s // y_count * y_count + (s + shift) % y_count) for s in range(seq_count)],
        )
        for shift in (1, 3, 2)
    ]
    returned = exchange(outgoing)
    query_grad, key_grad, value_grad = pl.pallas_call(
        functools.partial(final_kernel, slots=place_of),
        in_specs=[whole] * 4,
        out_specs=[hbm] * 3,
        out_shape=[pltpu.HBM((tokens, channels), BF16)] * 3,
        scratch_shapes=[token_tile] * 3 + [pltpu.SemaphoreType.DMA((3, CHUNKS))],
        compiler_params=pltpu.CompilerParams(vmem_limit_bytes=SMALL_LIMIT),
        name="products",
    )(returned, *tokens_in[1:])
    filter_grad = pl.pallas_call(
        functools.partial(spread_kernel, scale=1.0 / math.sqrt(length * seq_count)),
        in_specs=[scalars] + [whole] * 4 + [hbm],
        out_specs=hbm,
        out_shape=pltpu.HBM((length, 2 * LANES), F32),
        scratch_shapes=[
            pltpu.VMEM((y_count, length // 2, LANES), BF16),
            pltpu.VMEM((length, 2 * LANES), F32),
            pltpu.SemaphoreType.DMA((2, CHUNKS)),
        ],
        compiler_params=pltpu.CompilerParams(vmem_limit_bytes=SMALL_LIMIT),
        name="spread",
    )(place, summed, *others, pltpu.with_memory_space_constraint(query_grad, pltpu.HBM))
    return (
        query_grad.reshape(queries.shape),
        key_grad.reshape(queries.shape),
        value_grad.reshape(queries.shape),
        filter_grad,
    )


def solution(mesh):
    return jax.shard_map(
        functools.partial(local, ctx_count=mesh.shape["ctx"], seq_count=mesh.shape["seq"]),
        mesh=mesh,
        in_specs=(
            P("seq", "ctx", None),
            P("seq", "ctx", None),
            P("seq", "ctx", None),
            P("seq", "ctx", None),
            P(None, "ctx"),
        ),
        out_specs=(
            P("seq", "ctx", None),
            P("seq", "ctx", None),
            P("seq", "ctx", None),
            P(None, "ctx"),
        ),
        check_vma=False,
    )
```

```python
import functools
import math
import random

import jax
import jax.numpy as jnp
import numpy as np
from jax import lax
from jax.experimental import pallas as pl
from jax.experimental.pallas import tpu as pltpu
from jax.sharding import PartitionSpec as P

BLOCK = 256
HALF = 64
LANES = 128
F32 = jnp.float32
BF16 = jnp.bfloat16
TILE = 16
CHUNKS = 4
VMEM_LIMIT = 24 * 1024 * 1024
SMALL_LIMIT = 12 * 1024 * 1024


def member_order(y_count, ctx_count, together):
    draw = random.Random(31)
    runs = list(range(ctx_count // together))
    draw.shuffle(runs)
    order = []
    for run in runs:
        members = [y * ctx_count + run * together + c for y in range(y_count) for c in range(together)]
        draw.shuffle(members)
        order += members
    return order


def dft_tables():
    freq = np.arange(BLOCK)[:, None] * 2 + 1
    time = np.arange(BLOCK)[None, :]
    angle = (freq * time % (4 * BLOCK)) * (2.0 * math.pi / (4 * BLOCK))
    forward = np.concatenate((np.cos(angle), -np.sin(angle)), axis=0).astype(np.float32)
    upper = forward.astype(jnp.bfloat16)
    lower = (forward - upper.astype(np.float32)).astype(jnp.bfloat16)
    inverse = (forward.T / BLOCK).astype(jnp.bfloat16)
    return upper, lower, inverse


def low_lanes(shape):
    return lax.broadcasted_iota(jnp.int32, shape, len(shape) - 1) < HALF


def swap_halves(first, second):
    mask = low_lanes(first.shape)
    return (
        jnp.where(mask, first, pltpu.roll(second, HALF, 1)),
        jnp.where(mask, pltpu.roll(first, HALF, 1), second),
    )


def row_signs(shape):
    row = lax.broadcasted_iota(jnp.int32, shape, 0)
    return (1 - 2 * (row % 2)).astype(F32)


def gate_kernel(
    q_hbm, k_hbm, v_hbm, u_hbm, out_hbm,
    q_ref, k_ref, v_ref, u_ref, out_ref, in_sem, out_sem, *, slots
):
    half_rows = out_ref.shape[2]
    together = BLOCK // (2 * half_rows)
    width = q_ref.shape[1] // CHUNKS
    count = width // BLOCK
    sources = ((q_hbm, q_ref), (k_hbm, k_ref), (v_hbm, v_ref), (u_hbm, u_ref))
    loads = [load_chunk(sources, in_sem, chunk, width) for chunk in range(CHUNKS)]
    for row in loads:
        for copy in row:
            copy.start()
    stores = []
    for chunk in range(CHUNKS):
        for copy in loads[chunk]:
            copy.wait()

        for block in range(chunk * count, (chunk + 1) * count):
            for pair in range(2):
                lanes = pl.ds((block * 2 + pair) * LANES, LANES)
                kv = k_ref[:, lanes].astype(F32) * v_ref[:, lanes].astype(F32)
                gg = u_ref[:, lanes].astype(F32) * q_ref[:, lanes].astype(F32)
                for signal, value in enumerate((kv, gg)):
                    value = value.astype(BF16)
                    parts = swap_halves(value[:half_rows], value[half_rows:])
                    for odd in range(2):
                        out_ref[slots[2 * pair + odd][block], signal] = parts[odd]
            if block % together == together - 1:
                stores.append(send_run(out_ref, out_hbm, out_sem, slots, block // together, together))
    for copy in stores:
        copy.wait()


def send_run(source, target, sem, slots, run, together):
    places = [row[run * together + c] for row in slots for c in range(together)]
    part = pl.ds(min(places), len(places))
    copy = pltpu.make_async_copy(source.at[part], target.at[part], sem.at[run])
    copy.start()
    return copy


def load_chunk(pairs, sem, chunk, width):
    lanes = pl.ds(chunk * width, width)
    return [
        pltpu.make_async_copy(source.at[:, lanes], target.at[:, lanes], sem.at[which, chunk])
        for which, (source, target) in enumerate(pairs)
    ]


def filter_kernel(place_ref, taps_ref, upper_ref, lower_ref, out_ref):
    blocks = out_ref.shape[1]
    odd = place_ref[0] % 2
    signs = row_signs((BLOCK, LANES))
    mask = low_lanes((BLOCK, LANES))
    before = None
    for block in range(blocks):
        taps = taps_ref[pl.ds(block * BLOCK, BLOCK), :]
        turned = pltpu.roll(taps, HALF, 1)
        taps = jnp.where(jnp.logical_xor(mask, odd == 1), taps, turned)
        high = taps.astype(BF16)
        low = (taps - high.astype(F32)).astype(BF16)
        spec = jnp.dot(upper_ref[...], high, preferred_element_type=F32)
        spec = spec + jnp.dot(upper_ref[...], low, preferred_element_type=F32)
        spec = spec + jnp.dot(lower_ref[...], high, preferred_element_type=F32)
        real, imag = spec[:BLOCK], spec[BLOCK:]
        after = (real, imag)
        if before is not None:
            real, imag = real - signs * before[1], imag + signs * before[0]
        out_ref[0, block] = real
        out_ref[1, block] = imag
        before = after


def spectrum(arrived_ref, forward_ref, sig_ref, spec_ref, slots, signal):
    half_rows = arrived_ref.shape[2]
    per_block = BLOCK // (2 * half_rows)
    for block in range(spec_ref.shape[0]):
        for part in range(per_block):
            for pair in range(2):
                lanes = pl.ds(pair * LANES, LANES)
                first, second = swap_halves(
                    *(
                        arrived_ref[slots[2 * pair + odd][block * per_block + part], signal]
                        for odd in range(2)
                    )
                )
                at = part * 2 * half_rows
                sig_ref[block, pl.ds(at, half_rows), lanes] = first
                sig_ref[block, pl.ds(at + half_rows, half_rows), lanes] = second
        spec_ref[block] = jnp.dot(forward_ref[...], sig_ref[block], preferred_element_type=F32)


def total(terms):
    out = None
    for term in terms:
        out = term if out is None else out + term
    return out


def side(real, imag):
    return real, imag - real, real + imag


def multiply(pairs):
    first, second, third = (total([h[i] * x[i] for h, x in pairs]) for i in range(3))
    return first - third, first + second


def multiply_conj(pairs):
    first, second, third = (total([h[i] * x[i] for h, x in pairs]) for i in range(3))
    return first + third, first + second


def tile_slices(step):
    row = pl.multiple_of((step // 2) * TILE, TILE)
    lanes = pl.ds(pl.multiple_of((step % 2) * LANES, LANES), LANES)
    return pl.ds(row, TILE), pl.ds(BLOCK + row, TILE), lanes


def read_tiles(spec_ref, where):
    real_rows, imag_rows, lanes = where
    return [
        (spec_ref[b, real_rows, lanes], spec_ref[b, imag_rows, lanes]) for b in range(spec_ref.shape[0])
    ]


def write_tile(prod_ref, where, block, value):
    real_rows, imag_rows, lanes = where
    prod_ref[block, real_rows, lanes] = value[0].astype(BF16)
    prod_ref[block, imag_rows, lanes] = value[1].astype(BF16)


def cross_kernel(
    arrived_ref, forward_ref, inverse_ref, filt_hbm, terms_ref, value_ref, grad_ref, filt_ref,
    sig_ref, prod_ref, filt_sem, *, slots
):
    blocks = value_ref.shape[0]
    loads = filter_loads(filt_hbm, filt_ref, filt_sem)
    spectrum(arrived_ref, forward_ref, sig_ref, value_ref, slots, 0)
    spectrum(arrived_ref, forward_ref, sig_ref, grad_ref, slots, 1)
    half = blocks // 2
    signs = row_signs((TILE, LANES))

    def cross_terms(where):
        value, grad = read_tiles(value_ref, where), read_tiles(grad_ref, where)
        window = [
            (grad[b][0] + signs * grad[b + 1][1], grad[b][1] - signs * grad[b + 1][0])
            for b in range(blocks - 1)
        ] + [grad[-1]]
        left = [(real - imag, real, imag) for real, imag in value]
        right = [side(*x) for x in window]
        return [
            multiply_conj([(left[j], right[b + j]) for j in range(blocks - b)]) for b in range(blocks)
        ]

    def tile(step, carry):
        first, second = (cross_terms(tile_slices(2 * step + pair)) for pair in range(2))
        real_rows, imag_rows, _ = tile_slices(2 * step)
        for b in range(blocks):
            lanes = pl.ds(b // half * LANES, LANES)
            real, imag = (first[b][i] + second[b][i] for i in range(2))
            write_tile(prod_ref, (real_rows, imag_rows, lanes), b % half, (real, imag))
        return carry

    lax.fori_loop(0, BLOCK // TILE, tile, 0)

    mask = low_lanes((BLOCK, LANES))
    for block in range(half):
        cross = jnp.dot(inverse_ref[...], prod_ref[block], preferred_element_type=F32)
        early, late = (
            part + pltpu.roll(part, HALF, 1) for part in (cross[:, :LANES], cross[:, LANES:])
        )
        terms_ref[pl.ds(block * BLOCK, BLOCK), :] = jnp.where(mask, early, late).astype(BF16)
    for copy in loads:
        copy.wait()


def filter_loads(filt_hbm, filt_ref, sem):
    copies = [
        pltpu.make_async_copy(filt_hbm.at[kind, block], filt_ref.at[kind, block], sem.at[kind, block])
        for block in range(filt_ref.shape[1])
        for kind in range(2)
    ]
    for copy in copies:
        copy.start()
    return copies


def invert_block(inverse_ref, prod_ref, out_ref, block, slots, signal):
    half_rows = out_ref.shape[2]
    per_block = BLOCK // (2 * half_rows)
    result = jnp.dot(inverse_ref[...], prod_ref[block], preferred_element_type=F32).astype(BF16)
    for part in range(per_block):
        at = part * 2 * half_rows
        for pair in range(2):
            lanes = slice(pair * LANES, (pair + 1) * LANES)
            parts = swap_halves(
                result[at : at + half_rows, lanes], result[at + half_rows : at + 2 * half_rows, lanes]
            )
            for odd in range(2):
                place = slots[2 * pair + odd][block * per_block + part]
                out_ref[place, signal] = parts[odd]


def conv_kernel(
    value_ref, grad_ref, filt_ref, inverse_ref, out_hbm, conv_ref, back_ref, out_ref, out_sem, *, slots
):
    blocks = value_ref.shape[0]
    together = BLOCK // (2 * out_ref.shape[2])

    def tile(step, carry):
        where = tile_slices(step)
        rows = where[0]
        filt = [(filt_ref[0, b, rows, :], filt_ref[1, b, rows, :]) for b in range(blocks)]
        left = [(real + imag, real, imag) for real, imag in filt]
        right = [side(*x) for x in read_tiles(value_ref, where)]
        for b in range(blocks):
            write_tile(conv_ref, where, b, multiply([(left[j], right[b - j]) for j in range(b + 1)]))
        left = [(real - imag, real, imag) for real, imag in filt]
        right = [side(*x) for x in read_tiles(grad_ref, where)]
        for b in range(blocks):
            write_tile(
                back_ref, where, b, multiply_conj([(left[j], right[b + j]) for j in range(blocks - b)])
            )
        return carry

    lax.fori_loop(0, BLOCK // TILE * 2, tile, 0)
    stores = []
    for block in range(blocks):
        for signal, prod_ref in enumerate((conv_ref, back_ref)):
            invert_block(inverse_ref, prod_ref, out_ref, block, slots, signal)
        stores.append(send_run(out_ref, out_hbm, out_sem, slots, block, together))
    for copy in stores:
        copy.wait()


def final_kernel(
    ret_ref, k_ref, v_ref, u_ref, dq_hbm, dk_hbm, dv_hbm, dq_ref, dk_ref, dv_ref, out_sem, *, slots
):
    half_rows = ret_ref.shape[2]
    width = k_ref.shape[1] // CHUNKS
    count = width // BLOCK
    targets = ((dq_ref, dq_hbm), (dk_ref, dk_hbm), (dv_ref, dv_hbm))
    stores = [load_chunk(targets, out_sem, chunk, width) for chunk in range(CHUNKS)]
    for chunk in range(CHUNKS):
        for block in range(chunk * count, (chunk + 1) * count):
            for pair in range(2):
                lanes = pl.ds((block * 2 + pair) * LANES, LANES)
                conv, back = (
                    swap_halves(
                        *(ret_ref[slots[2 * pair + odd][block], signal] for odd in range(2))
                    )
                    for signal in range(2)
                )
                for part in range(2):
                    rows = pl.ds(part * half_rows, half_rows)
                    dq_ref[rows, lanes] = (u_ref[rows, lanes].astype(F32) * conv[part].astype(F32)).astype(BF16)
                    dk_ref[rows, lanes] = (back[part].astype(F32) * v_ref[rows, lanes].astype(F32)).astype(BF16)
                    dv_ref[rows, lanes] = (back[part].astype(F32) * k_ref[rows, lanes].astype(F32)).astype(BF16)
        for copy in stores[chunk]:
            copy.start()
    for row in stores:
        for copy in row:
            copy.wait()


def spread_kernel(
    place_ref, own_ref, up_ref, down_ref, far_ref, after_ref,
    out_hbm, held_ref, out_ref, out_sem, *, scale
):
    count = held_ref.shape[0]
    rows = held_ref.shape[1]
    step = rows // CHUNKS
    place = place_ref[0]
    for ref, shift in ((own_ref, 0), (up_ref, 1), (down_ref, 3), (far_ref, 2)):
        held_ref[lax.rem(place + count - shift, count)] = ref[...]
    stores = []
    for chunk in range(CHUNKS):
        part = pl.ds(chunk * step, step)
        for pair in range(2):
            lanes = pl.ds(pair * LANES, LANES)
            values = swap_halves(held_ref[2 * pair, part], held_ref[2 * pair + 1, part])
            for half in range(2):
                out_ref[pl.ds(half * rows + chunk * step, step), lanes] = values[half].astype(F32) * scale
        for half in range(2):
            part = pl.ds(half * rows + chunk * step, step)
            copy = pltpu.make_async_copy(out_ref.at[part], out_hbm.at[part], out_sem.at[half, chunk])
            copy.start()
            stores.append(copy)
    for copy in stores:
        copy.wait()


def local(queries, keys_in, value_in, upstream, filter_taps, *, ctx_count, seq_count):
    tokens, channels = queries.shape[1], queries.shape[2]
    length = filter_taps.shape[0]
    blocks = length // BLOCK
    y_count = 4
    z_count = seq_count // y_count
    half_rows = tokens // 2
    tokens_in = [a.reshape(tokens, channels) for a in (queries, keys_in, value_in, upstream)]
    params = pltpu.CompilerParams(vmem_limit_bytes=VMEM_LIMIT)
    upper, lower, inverse = (jnp.asarray(t) for t in dft_tables())
    members = y_count * ctx_count
    order = member_order(y_count, ctx_count, BLOCK // tokens)
    groups = [[z * members + m for m in order] for z in range(z_count)]
    place_of = [[order.index(y * ctx_count + c) for c in range(ctx_count)] for y in range(y_count)]
    hbm = pl.BlockSpec(memory_space=pltpu.HBM)
    whole = pl.BlockSpec(memory_space=pltpu.VMEM)
    scalars = pl.BlockSpec(memory_space=pltpu.SMEM)
    token_tile = pltpu.VMEM((tokens, channels), BF16)
    packed_shape = (members, 2, half_rows, LANES)

    packed = pl.pallas_call(
        functools.partial(gate_kernel, slots=place_of),
        in_specs=[hbm] * 4,
        out_specs=hbm,
        out_shape=pltpu.HBM(packed_shape, BF16),
        scratch_shapes=[token_tile] * 4
        + [
            pltpu.VMEM(packed_shape, BF16),
            pltpu.SemaphoreType.DMA((4, CHUNKS)),
            pltpu.SemaphoreType.DMA((blocks,)),
        ],
        compiler_params=params,
        name="gate",
    )(*(pltpu.with_memory_space_constraint(a, pltpu.HBM) for a in tokens_in))

    def exchange(array):
        return lax.all_to_all(array, ("seq", "ctx"), 0, 0, tiled=True, axis_index_groups=groups)

    arrived = exchange(packed)

    place = lax.rem(lax.axis_index("seq"), y_count).astype(jnp.int32).reshape(1)
    filt = pl.pallas_call(
        filter_kernel,
        grid_spec=pltpu.PrefetchScalarGridSpec(
            num_scalar_prefetch=1,
            grid=(1,),
            in_specs=[
                pl.BlockSpec((length, LANES), lambda i, place: (0, place[0] // 2)),
                pl.BlockSpec((2 * BLOCK, BLOCK), lambda i, place: (0, 0)),
                pl.BlockSpec((2 * BLOCK, BLOCK), lambda i, place: (0, 0)),
            ],
            out_specs=pl.BlockSpec((2, blocks, BLOCK, LANES), lambda i, place: (0, 0, 0, 0)),
        ),
        out_shape=pltpu.HBM((2, blocks, BLOCK, LANES), F32),
        compiler_params=params,
        name="filter_spectra",
    )(place, filter_taps, upper, lower)
    filt = pltpu.with_memory_space_constraint(filt, pltpu.HBM)

    signal_tile = pltpu.VMEM((blocks, BLOCK, 2 * LANES), BF16)
    product_tile = pltpu.VMEM((blocks, 2 * BLOCK, 2 * LANES), BF16)
    spectrum_shape = jax.ShapeDtypeStruct((blocks, 2 * BLOCK, 2 * LANES), F32)
    part_grad, value_spec, grad_spec, filt = pl.pallas_call(
        functools.partial(cross_kernel, slots=place_of),
        in_specs=[whole] * 3 + [hbm],
        out_specs=[whole] * 4,
        out_shape=[
            jax.ShapeDtypeStruct((length // 2, LANES), BF16),
            spectrum_shape,
            spectrum_shape,
            jax.ShapeDtypeStruct(filt.shape, F32),
        ],
        scratch_shapes=[
            signal_tile,
            pltpu.VMEM((blocks // 2, 2 * BLOCK, 2 * LANES), BF16),
            pltpu.SemaphoreType.DMA((2, blocks)),
        ],
        compiler_params=params,
        name="filter_terms",
    )(arrived, upper, inverse, filt)
    outgoing = pl.pallas_call(
        functools.partial(conv_kernel, slots=place_of),
        in_specs=[whole] * 4,
        out_specs=hbm,
        out_shape=pltpu.HBM(packed_shape, BF16),
        scratch_shapes=[
            product_tile,
            product_tile,
            pltpu.VMEM(packed_shape, BF16),
            pltpu.SemaphoreType.DMA((blocks,)),
        ],
        compiler_params=params,
        name="convolve",
    )(value_spec, grad_spec, filt, inverse)
    swapped = lax.ppermute(
        part_grad, "seq", [(s, (s + y_count) % seq_count) for s in range(seq_count)]
    )
    summed = (part_grad.astype(F32) + swapped.astype(F32)).astype(BF16)
    outgoing, summed = lax.optimization_barrier((outgoing, summed))
    others = [
        lax.ppermute(
            summed,
            "seq",
            [(s, s // y_count * y_count + (s + shift) % y_count) for s in range(seq_count)],
        )
        for shift in (1, 3, 2)
    ]
    returned = exchange(outgoing)
    query_grad, key_grad, value_grad = pl.pallas_call(
        functools.partial(final_kernel, slots=place_of),
        in_specs=[whole] * 4,
        out_specs=[hbm] * 3,
        out_shape=[pltpu.HBM((tokens, channels), BF16)] * 3,
        scratch_shapes=[token_tile] * 3 + [pltpu.SemaphoreType.DMA((3, CHUNKS))],
        compiler_params=pltpu.CompilerParams(vmem_limit_bytes=SMALL_LIMIT),
        name="products",
    )(returned, *tokens_in[1:])
    filter_grad = pl.pallas_call(
        functools.partial(spread_kernel, scale=1.0 / math.sqrt(length * seq_count)),
        in_specs=[scalars] + [whole] * 4 + [hbm],
        out_specs=hbm,
        out_shape=pltpu.HBM((length, 2 * LANES), F32),
        scratch_shapes=[
            pltpu.VMEM((y_count, length // 2, LANES), BF16),
            pltpu.VMEM((length, 2 * LANES), F32),
            pltpu.SemaphoreType.DMA((2, CHUNKS)),
        ],
        compiler_params=pltpu.CompilerParams(vmem_limit_bytes=SMALL_LIMIT),
        name="spread",
    )(place, summed, *others, pltpu.with_memory_space_constraint(query_grad, pltpu.HBM))
    return (
        query_grad.reshape(queries.shape),
        key_grad.reshape(queries.shape),
        value_grad.reshape(queries.shape),
        filter_grad,
    )


def solution(mesh):
    return jax.shard_map(
        functools.partial(local, ctx_count=mesh.shape["ctx"], seq_count=mesh.shape["seq"]),
        mesh=mesh,
        in_specs=(
            P("seq", "ctx", None),
            P("seq", "ctx", None),
            P("seq", "ctx", None),
            P("seq", "ctx", None),
            P(None, "ctx"),
        ),
        out_specs=(
            P("seq", "ctx", None),
            P("seq", "ctx", None),
            P("seq", "ctx", None),
            P(None, "ctx"),
        ),
        check_vma=False,
    )
```

```python
import functools
import math
import random

import jax
import jax.numpy as jnp
import numpy as np
from jax import lax
from jax.experimental import pallas as pl
from jax.experimental.pallas import tpu as pltpu
from jax.sharding import PartitionSpec as P

BLOCK = 256
HALF = 64
LANES = 128
F32 = jnp.float32
BF16 = jnp.bfloat16
TILE = 16
CHUNKS = 4
VMEM_LIMIT = 24 * 1024 * 1024
SMALL_LIMIT = 12 * 1024 * 1024


def member_order(y_count, ctx_count, together):
    draw = random.Random(44)
    runs = list(range(ctx_count // together))
    draw.shuffle(runs)
    order = []
    for run in runs:
        members = [y * ctx_count + run * together + c for y in range(y_count) for c in range(together)]
        draw.shuffle(members)
        order += members
    return order


def dft_tables():
    freq = np.arange(BLOCK)[:, None] * 2 + 1
    time = np.arange(BLOCK)[None, :]
    angle = (freq * time % (4 * BLOCK)) * (2.0 * math.pi / (4 * BLOCK))
    forward = np.concatenate((np.cos(angle), -np.sin(angle)), axis=0).astype(np.float32)
    upper = forward.astype(jnp.bfloat16)
    lower = (forward - upper.astype(np.float32)).astype(jnp.bfloat16)
    inverse = (forward.T / BLOCK).astype(jnp.bfloat16)
    return upper, lower, inverse


def low_lanes(shape):
    return lax.broadcasted_iota(jnp.int32, shape, len(shape) - 1) < HALF


def swap_halves(first, second):
    mask = low_lanes(first.shape)
    return (
        jnp.where(mask, first, pltpu.roll(second, HALF, 1)),
        jnp.where(mask, pltpu.roll(first, HALF, 1), second),
    )


def row_signs(shape):
    row = lax.broadcasted_iota(jnp.int32, shape, 0)
    return (1 - 2 * (row % 2)).astype(F32)


def gate_kernel(
    q_hbm, k_hbm, v_hbm, u_hbm, out_hbm,
    q_ref, k_ref, v_ref, u_ref, out_ref, in_sem, out_sem, *, slots
):
    half_rows = out_ref.shape[2]
    together = BLOCK // (2 * half_rows)
    width = q_ref.shape[1] // CHUNKS
    count = width // BLOCK
    sources = ((q_hbm, q_ref), (k_hbm, k_ref), (v_hbm, v_ref), (u_hbm, u_ref))
    loads = [load_chunk(sources, in_sem, chunk, width) for chunk in range(CHUNKS)]
    for row in loads:
        for copy in row:
            copy.start()
    stores = []
    for chunk in range(CHUNKS):
        for copy in loads[chunk]:
            copy.wait()

        for block in range(chunk * count, (chunk + 1) * count):
            for pair in range(2):
                lanes = pl.ds((block * 2 + pair) * LANES, LANES)
                kv = k_ref[:, lanes].astype(F32) * v_ref[:, lanes].astype(F32)
                gg = u_ref[:, lanes].astype(F32) * q_ref[:, lanes].astype(F32)
                for signal, value in enumerate((kv, gg)):
                    value = value.astype(BF16)
                    parts = swap_halves(value[:half_rows], value[half_rows:])
                    for odd in range(2):
                        out_ref[slots[2 * pair + odd][block], signal] = parts[odd]
            if block % together == together - 1:
                stores.append(send_run(out_ref, out_hbm, out_sem, slots, block // together, together))
    for copy in stores:
        copy.wait()


def send_run(source, target, sem, slots, run, together):
    places = [row[run * together + c] for row in slots for c in range(together)]
    part = pl.ds(min(places), len(places))
    copy = pltpu.make_async_copy(source.at[part], target.at[part], sem.at[run])
    copy.start()
    return copy


def load_chunk(pairs, sem, chunk, width):
    lanes = pl.ds(chunk * width, width)
    return [
        pltpu.make_async_copy(source.at[:, lanes], target.at[:, lanes], sem.at[which, chunk])
        for which, (source, target) in enumerate(pairs)
    ]


def filter_kernel(place_ref, taps_ref, upper_ref, lower_ref, out_ref):
    blocks = out_ref.shape[1]
    odd = place_ref[0] % 2
    signs = row_signs((BLOCK, LANES))
    mask = low_lanes((BLOCK, LANES))
    before = None
    for block in range(blocks):
        taps = taps_ref[pl.ds(block * BLOCK, BLOCK), :]
        turned = pltpu.roll(taps, HALF, 1)
        taps = jnp.where(jnp.logical_xor(mask, odd == 1), taps, turned)
        high = taps.astype(BF16)
        low = (taps - high.astype(F32)).astype(BF16)
        spec = jnp.dot(upper_ref[...], high, preferred_element_type=F32)
        spec = spec + jnp.dot(upper_ref[...], low, preferred_element_type=F32)
        spec = spec + jnp.dot(lower_ref[...], high, preferred_element_type=F32)
        real, imag = spec[:BLOCK], spec[BLOCK:]
        after = (real, imag)
        if before is not None:
            real, imag = real - signs * before[1], imag + signs * before[0]
        out_ref[0, block] = real
        out_ref[1, block] = imag
        before = after


def spectrum(arrived_ref, forward_ref, sig_ref, spec_ref, slots, signal):
    half_rows = arrived_ref.shape[2]
    per_block = BLOCK // (2 * half_rows)
    for block in range(spec_ref.shape[0]):
        for part in range(per_block):
            for pair in range(2):
                lanes = pl.ds(pair * LANES, LANES)
                first, second = swap_halves(
                    *(
                        arrived_ref[slots[2 * pair + odd][block * per_block + part], signal]
                        for odd in range(2)
                    )
                )
                at = part * 2 * half_rows
                sig_ref[block, pl.ds(at, half_rows), lanes] = first
                sig_ref[block, pl.ds(at + half_rows, half_rows), lanes] = second
        spec_ref[block] = jnp.dot(forward_ref[...], sig_ref[block], preferred_element_type=F32)


def total(terms):
    out = None
    for term in terms:
        out = term if out is None else out + term
    return out


def side(real, imag):
    return real, imag - real, real + imag


def multiply(pairs):
    first, second, third = (total([h[i] * x[i] for h, x in pairs]) for i in range(3))
    return first - third, first + second


def multiply_conj(pairs):
    first, second, third = (total([h[i] * x[i] for h, x in pairs]) for i in range(3))
    return first + third, first + second


def tile_slices(step):
    row = pl.multiple_of((step // 2) * TILE, TILE)
    lanes = pl.ds(pl.multiple_of((step % 2) * LANES, LANES), LANES)
    return pl.ds(row, TILE), pl.ds(BLOCK + row, TILE), lanes


def read_tiles(spec_ref, where):
    real_rows, imag_rows, lanes = where
    return [
        (spec_ref[b, real_rows, lanes], spec_ref[b, imag_rows, lanes]) for b in range(spec_ref.shape[0])
    ]


def write_tile(prod_ref, where, block, value):
    real_rows, imag_rows, lanes = where
    prod_ref[block, real_rows, lanes] = value[0].astype(BF16)
    prod_ref[block, imag_rows, lanes] = value[1].astype(BF16)


def cross_kernel(
    arrived_ref, forward_ref, inverse_ref, filt_hbm, terms_ref, value_ref, grad_ref, filt_ref,
    sig_ref, prod_ref, filt_sem, *, slots
):
    blocks = value_ref.shape[0]
    loads = filter_loads(filt_hbm, filt_ref, filt_sem)
    spectrum(arrived_ref, forward_ref, sig_ref, value_ref, slots, 0)
    spectrum(arrived_ref, forward_ref, sig_ref, grad_ref, slots, 1)
    half = blocks // 2
    signs = row_signs((TILE, LANES))

    def cross_terms(where):
        value, grad = read_tiles(value_ref, where), read_tiles(grad_ref, where)
        window = [
            (grad[b][0] + signs * grad[b + 1][1], grad[b][1] - signs * grad[b + 1][0])
            for b in range(blocks - 1)
        ] + [grad[-1]]
        left = [(real - imag, real, imag) for real, imag in value]
        right = [side(*x) for x in window]
        return [
            multiply_conj([(left[j], right[b + j]) for j in range(blocks - b)]) for b in range(blocks)
        ]

    def tile(step, carry):
        first, second = (cross_terms(tile_slices(2 * step + pair)) for pair in range(2))
        real_rows, imag_rows, _ = tile_slices(2 * step)
        for b in range(blocks):
            lanes = pl.ds(b // half * LANES, LANES)
            real, imag = (first[b][i] + second[b][i] for i in range(2))
            write_tile(prod_ref, (real_rows, imag_rows, lanes), b % half, (real, imag))
        return carry

    lax.fori_loop(0, BLOCK // TILE, tile, 0)

    mask = low_lanes((BLOCK, LANES))
    for block in range(half):
        cross = jnp.dot(inverse_ref[...], prod_ref[block], preferred_element_type=F32)
        early, late = (
            part + pltpu.roll(part, HALF, 1) for part in (cross[:, :LANES], cross[:, LANES:])
        )
        terms_ref[pl.ds(block * BLOCK, BLOCK), :] = jnp.where(mask, early, late).astype(BF16)
    for copy in loads:
        copy.wait()


def filter_loads(filt_hbm, filt_ref, sem):
    copies = [
        pltpu.make_async_copy(filt_hbm.at[kind, block], filt_ref.at[kind, block], sem.at[kind, block])
        for block in range(filt_ref.shape[1])
        for kind in range(2)
    ]
    for copy in copies:
        copy.start()
    return copies


def invert_block(inverse_ref, prod_ref, out_ref, block, slots, signal):
    half_rows = out_ref.shape[2]
    per_block = BLOCK // (2 * half_rows)
    result = jnp.dot(inverse_ref[...], prod_ref[block], preferred_element_type=F32).astype(BF16)
    for part in range(per_block):
        at = part * 2 * half_rows
        for pair in range(2):
            lanes = slice(pair * LANES, (pair + 1) * LANES)
            parts = swap_halves(
                result[at : at + half_rows, lanes], result[at + half_rows : at + 2 * half_rows, lanes]
            )
            for odd in range(2):
                place = slots[2 * pair + odd][block * per_block + part]
                out_ref[place, signal] = parts[odd]


def conv_kernel(
    value_ref, grad_ref, filt_ref, inverse_ref, out_hbm, conv_ref, back_ref, out_ref, out_sem, *, slots
):
    blocks = value_ref.shape[0]
    together = BLOCK // (2 * out_ref.shape[2])

    def tile(step, carry):
        where = tile_slices(step)
        rows = where[0]
        filt = [(filt_ref[0, b, rows, :], filt_ref[1, b, rows, :]) for b in range(blocks)]
        left = [(real + imag, real, imag) for real, imag in filt]
        right = [side(*x) for x in read_tiles(value_ref, where)]
        for b in range(blocks):
            write_tile(conv_ref, where, b, multiply([(left[j], right[b - j]) for j in range(b + 1)]))
        left = [(real - imag, real, imag) for real, imag in filt]
        right = [side(*x) for x in read_tiles(grad_ref, where)]
        for b in range(blocks):
            write_tile(
                back_ref, where, b, multiply_conj([(left[j], right[b + j]) for j in range(blocks - b)])
            )
        return carry

    lax.fori_loop(0, BLOCK // TILE * 2, tile, 0)
    stores = []
    for block in range(blocks):
        for signal, prod_ref in enumerate((conv_ref, back_ref)):
            invert_block(inverse_ref, prod_ref, out_ref, block, slots, signal)
        stores.append(send_run(out_ref, out_hbm, out_sem, slots, block, together))
    for copy in stores:
        copy.wait()


def final_kernel(
    ret_ref, k_ref, v_ref, u_ref, dq_hbm, dk_hbm, dv_hbm, dq_ref, dk_ref, dv_ref, out_sem, *, slots
):
    half_rows = ret_ref.shape[2]
    width = k_ref.shape[1] // CHUNKS
    count = width // BLOCK
    targets = ((dq_ref, dq_hbm), (dk_ref, dk_hbm), (dv_ref, dv_hbm))
    stores = [load_chunk(targets, out_sem, chunk, width) for chunk in range(CHUNKS)]
    for chunk in range(CHUNKS):
        for block in range(chunk * count, (chunk + 1) * count):
            for pair in range(2):
                lanes = pl.ds((block * 2 + pair) * LANES, LANES)
                conv, back = (
                    swap_halves(
                        *(ret_ref[slots[2 * pair + odd][block], signal] for odd in range(2))
                    )
                    for signal in range(2)
                )
                for part in range(2):
                    rows = pl.ds(part * half_rows, half_rows)
                    dq_ref[rows, lanes] = (u_ref[rows, lanes].astype(F32) * conv[part].astype(F32)).astype(BF16)
                    dk_ref[rows, lanes] = (back[part].astype(F32) * v_ref[rows, lanes].astype(F32)).astype(BF16)
                    dv_ref[rows, lanes] = (back[part].astype(F32) * k_ref[rows, lanes].astype(F32)).astype(BF16)
        for copy in stores[chunk]:
            copy.start()
    for row in stores:
        for copy in row:
            copy.wait()


def spread_kernel(
    place_ref, own_ref, up_ref, down_ref, far_ref, after_ref,
    out_hbm, held_ref, out_ref, out_sem, *, scale
):
    count = held_ref.shape[0]
    rows = held_ref.shape[1]
    step = rows // CHUNKS
    place = place_ref[0]
    for ref, shift in ((own_ref, 0), (up_ref, 1), (down_ref, 3), (far_ref, 2)):
        held_ref[lax.rem(place + count - shift, count)] = ref[...]
    stores = []
    for chunk in range(CHUNKS):
        part = pl.ds(chunk * step, step)
        for pair in range(2):
            lanes = pl.ds(pair * LANES, LANES)
            values = swap_halves(held_ref[2 * pair, part], held_ref[2 * pair + 1, part])
            for half in range(2):
                out_ref[pl.ds(half * rows + chunk * step, step), lanes] = values[half].astype(F32) * scale
        for half in range(2):
            part = pl.ds(half * rows + chunk * step, step)
            copy = pltpu.make_async_copy(out_ref.at[part], out_hbm.at[part], out_sem.at[half, chunk])
            copy.start()
            stores.append(copy)
    for copy in stores:
        copy.wait()


def local(queries, keys_in, value_in, upstream, filter_taps, *, ctx_count, seq_count):
    tokens, channels = queries.shape[1], queries.shape[2]
    length = filter_taps.shape[0]
    blocks = length // BLOCK
    y_count = 4
    z_count = seq_count // y_count
    half_rows = tokens // 2
    tokens_in = [a.reshape(tokens, channels) for a in (queries, keys_in, value_in, upstream)]
    params = pltpu.CompilerParams(vmem_limit_bytes=VMEM_LIMIT)
    upper, lower, inverse = (jnp.asarray(t) for t in dft_tables())
    members = y_count * ctx_count
    order = member_order(y_count, ctx_count, BLOCK // tokens)
    groups = [[z * members + m for m in order] for z in range(z_count)]
    place_of = [[order.index(y * ctx_count + c) for c in range(ctx_count)] for y in range(y_count)]
    hbm = pl.BlockSpec(memory_space=pltpu.HBM)
    whole = pl.BlockSpec(memory_space=pltpu.VMEM)
    scalars = pl.BlockSpec(memory_space=pltpu.SMEM)
    token_tile = pltpu.VMEM((tokens, channels), BF16)
    packed_shape = (members, 2, half_rows, LANES)

    packed = pl.pallas_call(
        functools.partial(gate_kernel, slots=place_of),
        in_specs=[hbm] * 4,
        out_specs=hbm,
        out_shape=pltpu.HBM(packed_shape, BF16),
        scratch_shapes=[token_tile] * 4
        + [
            pltpu.VMEM(packed_shape, BF16),
            pltpu.SemaphoreType.DMA((4, CHUNKS)),
            pltpu.SemaphoreType.DMA((blocks,)),
        ],
        compiler_params=params,
        name="gate",
    )(*(pltpu.with_memory_space_constraint(a, pltpu.HBM) for a in tokens_in))

    def exchange(array):
        return lax.all_to_all(array, ("seq", "ctx"), 0, 0, tiled=True, axis_index_groups=groups)

    arrived = exchange(packed)

    place = lax.rem(lax.axis_index("seq"), y_count).astype(jnp.int32).reshape(1)
    filt = pl.pallas_call(
        filter_kernel,
        grid_spec=pltpu.PrefetchScalarGridSpec(
            num_scalar_prefetch=1,
            grid=(1,),
            in_specs=[
                pl.BlockSpec((length, LANES), lambda i, place: (0, place[0] // 2)),
                pl.BlockSpec((2 * BLOCK, BLOCK), lambda i, place: (0, 0)),
                pl.BlockSpec((2 * BLOCK, BLOCK), lambda i, place: (0, 0)),
            ],
            out_specs=pl.BlockSpec((2, blocks, BLOCK, LANES), lambda i, place: (0, 0, 0, 0)),
        ),
        out_shape=pltpu.HBM((2, blocks, BLOCK, LANES), F32),
        compiler_params=params,
        name="filter_spectra",
    )(place, filter_taps, upper, lower)
    filt = pltpu.with_memory_space_constraint(filt, pltpu.HBM)

    signal_tile = pltpu.VMEM((blocks, BLOCK, 2 * LANES), BF16)
    product_tile = pltpu.VMEM((blocks, 2 * BLOCK, 2 * LANES), BF16)
    spectrum_shape = jax.ShapeDtypeStruct((blocks, 2 * BLOCK, 2 * LANES), F32)
    part_grad, value_spec, grad_spec, filt = pl.pallas_call(
        functools.partial(cross_kernel, slots=place_of),
        in_specs=[whole] * 3 + [hbm],
        out_specs=[whole] * 4,
        out_shape=[
            jax.ShapeDtypeStruct((length // 2, LANES), BF16),
            spectrum_shape,
            spectrum_shape,
            jax.ShapeDtypeStruct(filt.shape, F32),
        ],
        scratch_shapes=[
            signal_tile,
            pltpu.VMEM((blocks // 2, 2 * BLOCK, 2 * LANES), BF16),
            pltpu.SemaphoreType.DMA((2, blocks)),
        ],
        compiler_params=params,
        name="filter_terms",
    )(arrived, upper, inverse, filt)
    outgoing = pl.pallas_call(
        functools.partial(conv_kernel, slots=place_of),
        in_specs=[whole] * 4,
        out_specs=hbm,
        out_shape=pltpu.HBM(packed_shape, BF16),
        scratch_shapes=[
            product_tile,
            product_tile,
            pltpu.VMEM(packed_shape, BF16),
            pltpu.SemaphoreType.DMA((blocks,)),
        ],
        compiler_params=params,
        name="convolve",
    )(value_spec, grad_spec, filt, inverse)
    swapped = lax.ppermute(
        part_grad, "seq", [(s, (s + y_count) % seq_count) for s in range(seq_count)]
    )
    summed = (part_grad.astype(F32) + swapped.astype(F32)).astype(BF16)
    outgoing, summed = lax.optimization_barrier((outgoing, summed))
    others = [
        lax.ppermute(
            summed,
            "seq",
            [(s, s // y_count * y_count + (s + shift) % y_count) for s in range(seq_count)],
        )
        for shift in (1, 3, 2)
    ]
    returned = exchange(outgoing)
    query_grad, key_grad, value_grad = pl.pallas_call(
        functools.partial(final_kernel, slots=place_of),
        in_specs=[whole] * 4,
        out_specs=[hbm] * 3,
        out_shape=[pltpu.HBM((tokens, channels), BF16)] * 3,
        scratch_shapes=[token_tile] * 3 + [pltpu.SemaphoreType.DMA((3, CHUNKS))],
        compiler_params=pltpu.CompilerParams(vmem_limit_bytes=SMALL_LIMIT),
        name="products",
    )(returned, *tokens_in[1:])
    filter_grad = pl.pallas_call(
        functools.partial(spread_kernel, scale=1.0 / math.sqrt(length * seq_count)),
        in_specs=[scalars] + [whole] * 4 + [hbm],
        out_specs=hbm,
        out_shape=pltpu.HBM((length, 2 * LANES), F32),
        scratch_shapes=[
            pltpu.VMEM((y_count, length // 2, LANES), BF16),
            pltpu.VMEM((length, 2 * LANES), F32),
            pltpu.SemaphoreType.DMA((2, CHUNKS)),
        ],
        compiler_params=pltpu.CompilerParams(vmem_limit_bytes=SMALL_LIMIT),
        name="spread",
    )(place, summed, *others, pltpu.with_memory_space_constraint(query_grad, pltpu.HBM))
    return (
        query_grad.reshape(queries.shape),
        key_grad.reshape(queries.shape),
        value_grad.reshape(queries.shape),
        filter_grad,
    )


def solution(mesh):
    return jax.shard_map(
        functools.partial(local, ctx_count=mesh.shape["ctx"], seq_count=mesh.shape["seq"]),
        mesh=mesh,
        in_specs=(
            P("seq", "ctx", None),
            P("seq", "ctx", None),
            P("seq", "ctx", None),
            P("seq", "ctx", None),
            P(None, "ctx"),
        ),
        out_specs=(
            P("seq", "ctx", None),
            P("seq", "ctx", None),
            P("seq", "ctx", None),
            P(None, "ctx"),
        ),
        check_vma=False,
    )
```

```python
import functools
import math
import random

import jax
import jax.numpy as jnp
import numpy as np
from jax import lax
from jax.experimental import pallas as pl
from jax.experimental.pallas import tpu as pltpu
from jax.sharding import PartitionSpec as P

BLOCK = 256
HALF = 64
LANES = 128
F32 = jnp.float32
BF16 = jnp.bfloat16
TILE = 32
CHUNKS = 4
VMEM_LIMIT = 24 * 1024 * 1024
SMALL_LIMIT = 12 * 1024 * 1024


def member_order(y_count, ctx_count, together):
    draw = random.Random(44)
    runs = list(range(ctx_count // together))
    draw.shuffle(runs)
    order = []
    for run in runs:
        members = [y * ctx_count + run * together + c for y in range(y_count) for c in range(together)]
        draw.shuffle(members)
        order += members
    return order


def dft_tables():
    freq = np.arange(BLOCK)[:, None] * 2 + 1
    time = np.arange(BLOCK)[None, :]
    angle = (freq * time % (4 * BLOCK)) * (2.0 * math.pi / (4 * BLOCK))
    forward = np.concatenate((np.cos(angle), -np.sin(angle)), axis=0).astype(np.float32)
    upper = forward.astype(jnp.bfloat16)
    lower = (forward - upper.astype(np.float32)).astype(jnp.bfloat16)
    inverse = (forward.T / BLOCK).astype(jnp.bfloat16)
    return upper, lower, inverse


def low_lanes(shape):
    return lax.broadcasted_iota(jnp.int32, shape, len(shape) - 1) < HALF


def swap_halves(first, second):
    mask = low_lanes(first.shape)
    return (
        jnp.where(mask, first, pltpu.roll(second, HALF, 1)),
        jnp.where(mask, pltpu.roll(first, HALF, 1), second),
    )


def row_signs(shape):
    row = lax.broadcasted_iota(jnp.int32, shape, 0)
    return (1 - 2 * (row % 2)).astype(F32)


def gate_kernel(
    q_hbm, k_hbm, v_hbm, u_hbm, out_hbm,
    q_ref, k_ref, v_ref, u_ref, out_ref, in_sem, out_sem, *, slots
):
    half_rows = out_ref.shape[2]
    together = BLOCK // (2 * half_rows)
    width = q_ref.shape[1] // CHUNKS
    count = width // BLOCK
    sources = ((q_hbm, q_ref), (k_hbm, k_ref), (v_hbm, v_ref), (u_hbm, u_ref))
    loads = [load_chunk(sources, in_sem, chunk, width) for chunk in range(CHUNKS)]
    for row in loads:
        for copy in row:
            copy.start()
    stores = []
    for chunk in range(CHUNKS):
        for copy in loads[chunk]:
            copy.wait()

        for block in range(chunk * count, (chunk + 1) * count):
            for pair in range(2):
                lanes = pl.ds((block * 2 + pair) * LANES, LANES)
                kv = k_ref[:, lanes].astype(F32) * v_ref[:, lanes].astype(F32)
                gg = u_ref[:, lanes].astype(F32) * q_ref[:, lanes].astype(F32)
                for signal, value in enumerate((kv, gg)):
                    value = value.astype(BF16)
                    parts = swap_halves(value[:half_rows], value[half_rows:])
                    for odd in range(2):
                        out_ref[slots[2 * pair + odd][block], signal] = parts[odd]
            if block % together == together - 1:
                stores.append(send_run(out_ref, out_hbm, out_sem, slots, block // together, together))
    for copy in stores:
        copy.wait()


def send_run(source, target, sem, slots, run, together):
    places = [row[run * together + c] for row in slots for c in range(together)]
    part = pl.ds(min(places), len(places))
    copy = pltpu.make_async_copy(source.at[part], target.at[part], sem.at[run])
    copy.start()
    return copy


def load_chunk(pairs, sem, chunk, width):
    lanes = pl.ds(chunk * width, width)
    return [
        pltpu.make_async_copy(source.at[:, lanes], target.at[:, lanes], sem.at[which, chunk])
        for which, (source, target) in enumerate(pairs)
    ]


def filter_kernel(place_ref, taps_ref, upper_ref, lower_ref, out_ref):
    blocks = out_ref.shape[1]
    odd = place_ref[0] % 2
    signs = row_signs((BLOCK, LANES))
    mask = low_lanes((BLOCK, LANES))
    before = None
    for block in range(blocks):
        taps = taps_ref[pl.ds(block * BLOCK, BLOCK), :]
        turned = pltpu.roll(taps, HALF, 1)
        taps = jnp.where(jnp.logical_xor(mask, odd == 1), taps, turned)
        high = taps.astype(BF16)
        low = (taps - high.astype(F32)).astype(BF16)
        spec = jnp.dot(upper_ref[...], high, preferred_element_type=F32)
        spec = spec + jnp.dot(upper_ref[...], low, preferred_element_type=F32)
        spec = spec + jnp.dot(lower_ref[...], high, preferred_element_type=F32)
        real, imag = spec[:BLOCK], spec[BLOCK:]
        after = (real, imag)
        if before is not None:
            real, imag = real - signs * before[1], imag + signs * before[0]
        out_ref[0, block] = real
        out_ref[1, block] = imag
        before = after


def spectrum(arrived_ref, forward_ref, sig_ref, spec_ref, slots, signal):
    half_rows = arrived_ref.shape[2]
    per_block = BLOCK // (2 * half_rows)
    for block in range(spec_ref.shape[0]):
        for part in range(per_block):
            for pair in range(2):
                lanes = pl.ds(pair * LANES, LANES)
                first, second = swap_halves(
                    *(
                        arrived_ref[slots[2 * pair + odd][block * per_block + part], signal]
                        for odd in range(2)
                    )
                )
                at = part * 2 * half_rows
                sig_ref[block, pl.ds(at, half_rows), lanes] = first
                sig_ref[block, pl.ds(at + half_rows, half_rows), lanes] = second
        spec_ref[block] = jnp.dot(forward_ref[...], sig_ref[block], preferred_element_type=F32)


def total(terms):
    out = None
    for term in terms:
        out = term if out is None else out + term
    return out


def side(real, imag):
    return real, imag - real, real + imag


def multiply(pairs):
    first, second, third = (total([h[i] * x[i] for h, x in pairs]) for i in range(3))
    return first - third, first + second


def multiply_conj(pairs):
    first, second, third = (total([h[i] * x[i] for h, x in pairs]) for i in range(3))
    return first + third, first + second


def tile_slices(step):
    row = pl.multiple_of((step // 2) * TILE, TILE)
    lanes = pl.ds(pl.multiple_of((step % 2) * LANES, LANES), LANES)
    return pl.ds(row, TILE), pl.ds(BLOCK + row, TILE), lanes


def read_tiles(spec_ref, where):
    real_rows, imag_rows, lanes = where
    return [
        (spec_ref[b, real_rows, lanes], spec_ref[b, imag_rows, lanes]) for b in range(spec_ref.shape[0])
    ]


def write_tile(prod_ref, where, block, value):
    real_rows, imag_rows, lanes = where
    prod_ref[block, real_rows, lanes] = value[0].astype(BF16)
    prod_ref[block, imag_rows, lanes] = value[1].astype(BF16)


def cross_kernel(
    arrived_ref, forward_ref, inverse_ref, filt_hbm, terms_ref, value_ref, grad_ref, filt_ref,
    sig_ref, prod_ref, filt_sem, *, slots
):
    blocks = value_ref.shape[0]
    loads = filter_loads(filt_hbm, filt_ref, filt_sem)
    spectrum(arrived_ref, forward_ref, sig_ref, value_ref, slots, 0)
    spectrum(arrived_ref, forward_ref, sig_ref, grad_ref, slots, 1)
    half = blocks // 2
    signs = row_signs((TILE, LANES))

    def cross_terms(where):
        value, grad = read_tiles(value_ref, where), read_tiles(grad_ref, where)
        window = [
            (grad[b][0] + signs * grad[b + 1][1], grad[b][1] - signs * grad[b + 1][0])
            for b in range(blocks - 1)
        ] + [grad[-1]]
        left = [(real - imag, real, imag) for real, imag in value]
        right = [side(*x) for x in window]
        return [
            multiply_conj([(left[j], right[b + j]) for j in range(blocks - b)]) for b in range(blocks)
        ]

    def tile(step, carry):
        first, second = (cross_terms(tile_slices(2 * step + pair)) for pair in range(2))
        real_rows, imag_rows, _ = tile_slices(2 * step)
        for b in range(blocks):
            lanes = pl.ds(b // half * LANES, LANES)
            real, imag = (first[b][i] + second[b][i] for i in range(2))
            write_tile(prod_ref, (real_rows, imag_rows, lanes), b % half, (real, imag))
        return carry

    lax.fori_loop(0, BLOCK // TILE, tile, 0)

    mask = low_lanes((BLOCK, LANES))
    for block in range(half):
        cross = jnp.dot(inverse_ref[...], prod_ref[block], preferred_element_type=F32)
        early, late = (
            part + pltpu.roll(part, HALF, 1) for part in (cross[:, :LANES], cross[:, LANES:])
        )
        terms_ref[pl.ds(block * BLOCK, BLOCK), :] = jnp.where(mask, early, late).astype(BF16)
    for copy in loads:
        copy.wait()


def filter_loads(filt_hbm, filt_ref, sem):
    copies = [
        pltpu.make_async_copy(filt_hbm.at[kind, block], filt_ref.at[kind, block], sem.at[kind, block])
        for block in range(filt_ref.shape[1])
        for kind in range(2)
    ]
    for copy in copies:
        copy.start()
    return copies


def invert_block(inverse_ref, prod_ref, out_ref, block, slots, signal):
    half_rows = out_ref.shape[2]
    per_block = BLOCK // (2 * half_rows)
    result = jnp.dot(inverse_ref[...], prod_ref[block], preferred_element_type=F32).astype(BF16)
    for part in range(per_block):
        at = part * 2 * half_rows
        for pair in range(2):
            lanes = slice(pair * LANES, (pair + 1) * LANES)
            parts = swap_halves(
                result[at : at + half_rows, lanes], result[at + half_rows : at + 2 * half_rows, lanes]
            )
            for odd in range(2):
                place = slots[2 * pair + odd][block * per_block + part]
                out_ref[place, signal] = parts[odd]


def conv_kernel(
    value_ref, grad_ref, filt_ref, inverse_ref, out_hbm, conv_ref, back_ref, out_ref, out_sem, *, slots
):
    blocks = value_ref.shape[0]
    together = BLOCK // (2 * out_ref.shape[2])

    def tile(step, carry):
        where = tile_slices(step)
        rows = where[0]
        filt = [(filt_ref[0, b, rows, :], filt_ref[1, b, rows, :]) for b in range(blocks)]
        left = [(real + imag, real, imag) for real, imag in filt]
        right = [side(*x) for x in read_tiles(value_ref, where)]
        for b in range(blocks):
            write_tile(conv_ref, where, b, multiply([(left[j], right[b - j]) for j in range(b + 1)]))
        left = [(real - imag, real, imag) for real, imag in filt]
        right = [side(*x) for x in read_tiles(grad_ref, where)]
        for b in range(blocks):
            write_tile(
                back_ref, where, b, multiply_conj([(left[j], right[b + j]) for j in range(blocks - b)])
            )
        return carry

    lax.fori_loop(0, BLOCK // TILE * 2, tile, 0)
    stores = []
    for block in range(blocks):
        for signal, prod_ref in enumerate((conv_ref, back_ref)):
            invert_block(inverse_ref, prod_ref, out_ref, block, slots, signal)
        stores.append(send_run(out_ref, out_hbm, out_sem, slots, block, together))
    for copy in stores:
        copy.wait()


def final_kernel(
    ret_ref, k_ref, v_ref, u_ref, dq_hbm, dk_hbm, dv_hbm, dq_ref, dk_ref, dv_ref, out_sem, *, slots
):
    half_rows = ret_ref.shape[2]
    width = k_ref.shape[1] // CHUNKS
    count = width // BLOCK
    targets = ((dq_ref, dq_hbm), (dk_ref, dk_hbm), (dv_ref, dv_hbm))
    stores = [load_chunk(targets, out_sem, chunk, width) for chunk in range(CHUNKS)]
    for chunk in range(CHUNKS):
        for block in range(chunk * count, (chunk + 1) * count):
            for pair in range(2):
                lanes = pl.ds((block * 2 + pair) * LANES, LANES)
                conv, back = (
                    swap_halves(
                        *(ret_ref[slots[2 * pair + odd][block], signal] for odd in range(2))
                    )
                    for signal in range(2)
                )
                for part in range(2):
                    rows = pl.ds(part * half_rows, half_rows)
                    dq_ref[rows, lanes] = (u_ref[rows, lanes].astype(F32) * conv[part].astype(F32)).astype(BF16)
                    dk_ref[rows, lanes] = (back[part].astype(F32) * v_ref[rows, lanes].astype(F32)).astype(BF16)
                    dv_ref[rows, lanes] = (back[part].astype(F32) * k_ref[rows, lanes].astype(F32)).astype(BF16)
        for copy in stores[chunk]:
            copy.start()
    for row in stores:
        for copy in row:
            copy.wait()


def spread_kernel(
    place_ref, own_ref, up_ref, down_ref, far_ref, after_ref,
    out_hbm, held_ref, out_ref, out_sem, *, scale
):
    count = held_ref.shape[0]
    rows = held_ref.shape[1]
    step = rows // CHUNKS
    place = place_ref[0]
    for ref, shift in ((own_ref, 0), (up_ref, 1), (down_ref, 3), (far_ref, 2)):
        held_ref[lax.rem(place + count - shift, count)] = ref[...]
    stores = []
    for chunk in range(CHUNKS):
        part = pl.ds(chunk * step, step)
        for pair in range(2):
            lanes = pl.ds(pair * LANES, LANES)
            values = swap_halves(held_ref[2 * pair, part], held_ref[2 * pair + 1, part])
            for half in range(2):
                out_ref[pl.ds(half * rows + chunk * step, step), lanes] = values[half].astype(F32) * scale
        for half in range(2):
            part = pl.ds(half * rows + chunk * step, step)
            copy = pltpu.make_async_copy(out_ref.at[part], out_hbm.at[part], out_sem.at[half, chunk])
            copy.start()
            stores.append(copy)
    for copy in stores:
        copy.wait()


def local(queries, keys_in, value_in, upstream, filter_taps, *, ctx_count, seq_count):
    tokens, channels = queries.shape[1], queries.shape[2]
    length = filter_taps.shape[0]
    blocks = length // BLOCK
    y_count = 4
    z_count = seq_count // y_count
    half_rows = tokens // 2
    tokens_in = [a.reshape(tokens, channels) for a in (queries, keys_in, value_in, upstream)]
    params = pltpu.CompilerParams(vmem_limit_bytes=VMEM_LIMIT)
    upper, lower, inverse = (jnp.asarray(t) for t in dft_tables())
    members = y_count * ctx_count
    order = member_order(y_count, ctx_count, BLOCK // tokens)
    groups = [[z * members + m for m in order] for z in range(z_count)]
    place_of = [[order.index(y * ctx_count + c) for c in range(ctx_count)] for y in range(y_count)]
    hbm = pl.BlockSpec(memory_space=pltpu.HBM)
    whole = pl.BlockSpec(memory_space=pltpu.VMEM)
    scalars = pl.BlockSpec(memory_space=pltpu.SMEM)
    token_tile = pltpu.VMEM((tokens, channels), BF16)
    packed_shape = (members, 2, half_rows, LANES)

    packed = pl.pallas_call(
        functools.partial(gate_kernel, slots=place_of),
        in_specs=[hbm] * 4,
        out_specs=hbm,
        out_shape=pltpu.HBM(packed_shape, BF16),
        scratch_shapes=[token_tile] * 4
        + [
            pltpu.VMEM(packed_shape, BF16),
            pltpu.SemaphoreType.DMA((4, CHUNKS)),
            pltpu.SemaphoreType.DMA((blocks,)),
        ],
        compiler_params=params,
        name="gate",
    )(*(pltpu.with_memory_space_constraint(a, pltpu.HBM) for a in tokens_in))

    def exchange(array):
        return lax.all_to_all(array, ("seq", "ctx"), 0, 0, tiled=True, axis_index_groups=groups)

    arrived = exchange(packed)

    place = lax.rem(lax.axis_index("seq"), y_count).astype(jnp.int32).reshape(1)
    filt = pl.pallas_call(
        filter_kernel,
        grid_spec=pltpu.PrefetchScalarGridSpec(
            num_scalar_prefetch=1,
            grid=(1,),
            in_specs=[
                pl.BlockSpec((length, LANES), lambda i, place: (0, place[0] // 2)),
                pl.BlockSpec((2 * BLOCK, BLOCK), lambda i, place: (0, 0)),
                pl.BlockSpec((2 * BLOCK, BLOCK), lambda i, place: (0, 0)),
            ],
            out_specs=pl.BlockSpec((2, blocks, BLOCK, LANES), lambda i, place: (0, 0, 0, 0)),
        ),
        out_shape=pltpu.HBM((2, blocks, BLOCK, LANES), F32),
        compiler_params=params,
        name="filter_spectra",
    )(place, filter_taps, upper, lower)
    filt = pltpu.with_memory_space_constraint(filt, pltpu.HBM)

    signal_tile = pltpu.VMEM((blocks, BLOCK, 2 * LANES), BF16)
    product_tile = pltpu.VMEM((blocks, 2 * BLOCK, 2 * LANES), BF16)
    spectrum_shape = jax.ShapeDtypeStruct((blocks, 2 * BLOCK, 2 * LANES), F32)
    part_grad, value_spec, grad_spec, filt = pl.pallas_call(
        functools.partial(cross_kernel, slots=place_of),
        in_specs=[whole] * 3 + [hbm],
        out_specs=[whole] * 4,
        out_shape=[
            jax.ShapeDtypeStruct((length // 2, LANES), BF16),
            spectrum_shape,
            spectrum_shape,
            jax.ShapeDtypeStruct(filt.shape, F32),
        ],
        scratch_shapes=[
            signal_tile,
            pltpu.VMEM((blocks // 2, 2 * BLOCK, 2 * LANES), BF16),
            pltpu.SemaphoreType.DMA((2, blocks)),
        ],
        compiler_params=params,
        name="filter_terms",
    )(arrived, upper, inverse, filt)
    outgoing = pl.pallas_call(
        functools.partial(conv_kernel, slots=place_of),
        in_specs=[whole] * 4,
        out_specs=hbm,
        out_shape=pltpu.HBM(packed_shape, BF16),
        scratch_shapes=[
            product_tile,
            product_tile,
            pltpu.VMEM(packed_shape, BF16),
            pltpu.SemaphoreType.DMA((blocks,)),
        ],
        compiler_params=params,
        name="convolve",
    )(value_spec, grad_spec, filt, inverse)
    swapped = lax.ppermute(
        part_grad, "seq", [(s, (s + y_count) % seq_count) for s in range(seq_count)]
    )
    summed = (part_grad.astype(F32) + swapped.astype(F32)).astype(BF16)
    outgoing, summed = lax.optimization_barrier((outgoing, summed))
    others = [
        lax.ppermute(
            summed,
            "seq",
            [(s, s // y_count * y_count + (s + shift) % y_count) for s in range(seq_count)],
        )
        for shift in (1, 3, 2)
    ]
    returned = exchange(outgoing)
    query_grad, key_grad, value_grad = pl.pallas_call(
        functools.partial(final_kernel, slots=place_of),
        in_specs=[whole] * 4,
        out_specs=[hbm] * 3,
        out_shape=[pltpu.HBM((tokens, channels), BF16)] * 3,
        scratch_shapes=[token_tile] * 3 + [pltpu.SemaphoreType.DMA((3, CHUNKS))],
        compiler_params=pltpu.CompilerParams(vmem_limit_bytes=SMALL_LIMIT),
        name="products",
    )(returned, *tokens_in[1:])
    filter_grad = pl.pallas_call(
        functools.partial(spread_kernel, scale=1.0 / math.sqrt(length * seq_count)),
        in_specs=[scalars] + [whole] * 4 + [hbm],
        out_specs=hbm,
        out_shape=pltpu.HBM((length, 2 * LANES), F32),
        scratch_shapes=[
            pltpu.VMEM((y_count, length // 2, LANES), BF16),
            pltpu.VMEM((length, 2 * LANES), F32),
            pltpu.SemaphoreType.DMA((2, CHUNKS)),
        ],
        compiler_params=pltpu.CompilerParams(vmem_limit_bytes=SMALL_LIMIT),
        name="spread",
    )(place, summed, *others, pltpu.with_memory_space_constraint(query_grad, pltpu.HBM))
    return (
        query_grad.reshape(queries.shape),
        key_grad.reshape(queries.shape),
        value_grad.reshape(queries.shape),
        filter_grad,
    )


def solution(mesh):
    return jax.shard_map(
        functools.partial(local, ctx_count=mesh.shape["ctx"], seq_count=mesh.shape["seq"]),
        mesh=mesh,
        in_specs=(
            P("seq", "ctx", None),
            P("seq", "ctx", None),
            P("seq", "ctx", None),
            P("seq", "ctx", None),
            P(None, "ctx"),
        ),
        out_specs=(
            P("seq", "ctx", None),
            P("seq", "ctx", None),
            P("seq", "ctx", None),
            P(None, "ctx"),
        ),
        check_vma=False,
    )
```

```python
import functools
import math
import random

import jax
import jax.numpy as jnp
import numpy as np
from jax import lax
from jax.experimental import pallas as pl
from jax.experimental.pallas import tpu as pltpu
from jax.sharding import PartitionSpec as P

BLOCK = 256
HALF = 64
LANES = 128
F32 = jnp.float32
BF16 = jnp.bfloat16
TILE = 32
CHUNKS = 4
SPREAD_CHUNKS = 8
VMEM_LIMIT = 24 * 1024 * 1024
SMALL_LIMIT = 12 * 1024 * 1024


def member_order(y_count, ctx_count, together):
    draw = random.Random(44)
    runs = list(range(ctx_count // together))
    draw.shuffle(runs)
    order = []
    for run in runs:
        members = [y * ctx_count + run * together + c for y in range(y_count) for c in range(together)]
        draw.shuffle(members)
        order += members
    return order


def dft_tables():
    freq = np.arange(BLOCK)[:, None] * 2 + 1
    time = np.arange(BLOCK)[None, :]
    angle = (freq * time % (4 * BLOCK)) * (2.0 * math.pi / (4 * BLOCK))
    forward = np.concatenate((np.cos(angle), -np.sin(angle)), axis=0).astype(np.float32)
    upper = forward.astype(jnp.bfloat16)
    lower = (forward - upper.astype(np.float32)).astype(jnp.bfloat16)
    inverse = (forward.T / BLOCK).astype(jnp.bfloat16)
    return upper, lower, inverse


def low_lanes(shape):
    return lax.broadcasted_iota(jnp.int32, shape, len(shape) - 1) < HALF


def swap_halves(first, second):
    mask = low_lanes(first.shape)
    return (
        jnp.where(mask, first, pltpu.roll(second, HALF, 1)),
        jnp.where(mask, pltpu.roll(first, HALF, 1), second),
    )


def row_signs(shape):
    row = lax.broadcasted_iota(jnp.int32, shape, 0)
    return (1 - 2 * (row % 2)).astype(F32)


def gate_kernel(
    q_hbm, k_hbm, v_hbm, u_hbm, out_hbm,
    q_ref, k_ref, v_ref, u_ref, out_ref, in_sem, out_sem, *, slots
):
    half_rows = out_ref.shape[2]
    together = BLOCK // (2 * half_rows)
    width = q_ref.shape[1] // CHUNKS
    count = width // BLOCK
    sources = ((q_hbm, q_ref), (k_hbm, k_ref), (v_hbm, v_ref), (u_hbm, u_ref))
    loads = [load_chunk(sources, in_sem, chunk, width) for chunk in range(CHUNKS)]
    for row in loads:
        for copy in row:
            copy.start()
    stores = []
    for chunk in range(CHUNKS):
        for copy in loads[chunk]:
            copy.wait()

        for block in range(chunk * count, (chunk + 1) * count):
            for pair in range(2):
                lanes = pl.ds((block * 2 + pair) * LANES, LANES)
                kv = k_ref[:, lanes].astype(F32) * v_ref[:, lanes].astype(F32)
                gg = u_ref[:, lanes].astype(F32) * q_ref[:, lanes].astype(F32)
                for signal, value in enumerate((kv, gg)):
                    value = value.astype(BF16)
                    parts = swap_halves(value[:half_rows], value[half_rows:])
                    for odd in range(2):
                        out_ref[slots[2 * pair + odd][block], signal] = parts[odd]
            if block % together == together - 1:
                stores.append(send_run(out_ref, out_hbm, out_sem, slots, block // together, together))
    for copy in stores:
        copy.wait()


def send_run(source, target, sem, slots, run, together):
    places = [row[run * together + c] for row in slots for c in range(together)]
    part = pl.ds(min(places), len(places))
    copy = pltpu.make_async_copy(source.at[part], target.at[part], sem.at[run])
    copy.start()
    return copy


def load_chunk(pairs, sem, chunk, width):
    lanes = pl.ds(chunk * width, width)
    return [
        pltpu.make_async_copy(source.at[:, lanes], target.at[:, lanes], sem.at[which, chunk])
        for which, (source, target) in enumerate(pairs)
    ]


def filter_kernel(place_ref, taps_ref, upper_ref, lower_ref, out_ref):
    blocks = out_ref.shape[1]
    odd = place_ref[0] % 2
    signs = row_signs((BLOCK, LANES))
    mask = low_lanes((BLOCK, LANES))
    before = None
    for block in range(blocks):
        taps = taps_ref[pl.ds(block * BLOCK, BLOCK), :]
        turned = pltpu.roll(taps, HALF, 1)
        taps = jnp.where(jnp.logical_xor(mask, odd == 1), taps, turned)
        high = taps.astype(BF16)
        low = (taps - high.astype(F32)).astype(BF16)
        spec = jnp.dot(upper_ref[...], high, preferred_element_type=F32)
        spec = spec + jnp.dot(upper_ref[...], low, preferred_element_type=F32)
        spec = spec + jnp.dot(lower_ref[...], high, preferred_element_type=F32)
        real, imag = spec[:BLOCK], spec[BLOCK:]
        after = (real, imag)
        if before is not None:
            real, imag = real - signs * before[1], imag + signs * before[0]
        out_ref[0, block] = real
        out_ref[1, block] = imag
        before = after


def spectrum(arrived_ref, forward_ref, sig_ref, spec_ref, slots, signal):
    half_rows = arrived_ref.shape[2]
    per_block = BLOCK // (2 * half_rows)
    for block in range(spec_ref.shape[0]):
        for part in range(per_block):
            for pair in range(2):
                lanes = pl.ds(pair * LANES, LANES)
                first, second = swap_halves(
                    *(
                        arrived_ref[slots[2 * pair + odd][block * per_block + part], signal]
                        for odd in range(2)
                    )
                )
                at = part * 2 * half_rows
                sig_ref[block, pl.ds(at, half_rows), lanes] = first
                sig_ref[block, pl.ds(at + half_rows, half_rows), lanes] = second
        spec_ref[block] = jnp.dot(forward_ref[...], sig_ref[block], preferred_element_type=F32)


def total(terms):
    out = None
    for term in terms:
        out = term if out is None else out + term
    return out


def side(real, imag):
    return real, imag - real, real + imag


def multiply(pairs):
    first, second, third = (total([h[i] * x[i] for h, x in pairs]) for i in range(3))
    return first - third, first + second


def multiply_conj(pairs):
    first, second, third = (total([h[i] * x[i] for h, x in pairs]) for i in range(3))
    return first + third, first + second


def tile_slices(step):
    row = pl.multiple_of((step // 2) * TILE, TILE)
    lanes = pl.ds(pl.multiple_of((step % 2) * LANES, LANES), LANES)
    return pl.ds(row, TILE), pl.ds(BLOCK + row, TILE), lanes


def read_tiles(spec_ref, where):
    real_rows, imag_rows, lanes = where
    return [
        (spec_ref[b, real_rows, lanes], spec_ref[b, imag_rows, lanes]) for b in range(spec_ref.shape[0])
    ]


def write_tile(prod_ref, where, block, value):
    real_rows, imag_rows, lanes = where
    prod_ref[block, real_rows, lanes] = value[0].astype(BF16)
    prod_ref[block, imag_rows, lanes] = value[1].astype(BF16)


def cross_kernel(
    arrived_ref, forward_ref, inverse_ref, filt_hbm, terms_ref, value_ref, grad_ref, filt_ref,
    sig_ref, prod_ref, filt_sem, *, slots
):
    blocks = value_ref.shape[0]
    loads = filter_loads(filt_hbm, filt_ref, filt_sem)
    spectrum(arrived_ref, forward_ref, sig_ref, value_ref, slots, 0)
    spectrum(arrived_ref, forward_ref, sig_ref, grad_ref, slots, 1)
    half = blocks // 2
    signs = row_signs((TILE, LANES))

    def cross_terms(where):
        value, grad = read_tiles(value_ref, where), read_tiles(grad_ref, where)
        window = [
            (grad[b][0] + signs * grad[b + 1][1], grad[b][1] - signs * grad[b + 1][0])
            for b in range(blocks - 1)
        ] + [grad[-1]]
        left = [(real - imag, real, imag) for real, imag in value]
        right = [side(*x) for x in window]
        return [
            multiply_conj([(left[j], right[b + j]) for j in range(blocks - b)]) for b in range(blocks)
        ]

    def tile(step, carry):
        first, second = (cross_terms(tile_slices(2 * step + pair)) for pair in range(2))
        real_rows, imag_rows, _ = tile_slices(2 * step)
        for b in range(blocks):
            lanes = pl.ds(b // half * LANES, LANES)
            real, imag = (first[b][i] + second[b][i] for i in range(2))
            write_tile(prod_ref, (real_rows, imag_rows, lanes), b % half, (real, imag))
        return carry

    lax.fori_loop(0, BLOCK // TILE, tile, 0)

    mask = low_lanes((BLOCK, LANES))
    for block in range(half):
        cross = jnp.dot(inverse_ref[...], prod_ref[block], preferred_element_type=F32)
        early, late = (
            part + pltpu.roll(part, HALF, 1) for part in (cross[:, :LANES], cross[:, LANES:])
        )
        terms_ref[pl.ds(block * BLOCK, BLOCK), :] = jnp.where(mask, early, late).astype(BF16)
    for copy in loads:
        copy.wait()


def filter_loads(filt_hbm, filt_ref, sem):
    copies = [
        pltpu.make_async_copy(filt_hbm.at[kind, block], filt_ref.at[kind, block], sem.at[kind, block])
        for block in range(filt_ref.shape[1])
        for kind in range(2)
    ]
    for copy in copies:
        copy.start()
    return copies


def invert_block(inverse_ref, prod_ref, out_ref, block, slots, signal):
    half_rows = out_ref.shape[2]
    per_block = BLOCK // (2 * half_rows)
    result = jnp.dot(inverse_ref[...], prod_ref[block], preferred_element_type=F32).astype(BF16)
    for part in range(per_block):
        at = part * 2 * half_rows
        for pair in range(2):
            lanes = slice(pair * LANES, (pair + 1) * LANES)
            parts = swap_halves(
                result[at : at + half_rows, lanes], result[at + half_rows : at + 2 * half_rows, lanes]
            )
            for odd in range(2):
                place = slots[2 * pair + odd][block * per_block + part]
                out_ref[place, signal] = parts[odd]


def conv_kernel(
    value_ref, grad_ref, filt_ref, inverse_ref, out_hbm, conv_ref, back_ref, out_ref, out_sem, *, slots
):
    blocks = value_ref.shape[0]
    together = BLOCK // (2 * out_ref.shape[2])

    def tile(step, carry):
        where = tile_slices(step)
        rows = where[0]
        filt = [(filt_ref[0, b, rows, :], filt_ref[1, b, rows, :]) for b in range(blocks)]
        left = [(real + imag, real, imag) for real, imag in filt]
        right = [side(*x) for x in read_tiles(value_ref, where)]
        for b in range(blocks):
            write_tile(conv_ref, where, b, multiply([(left[j], right[b - j]) for j in range(b + 1)]))
        left = [(real - imag, real, imag) for real, imag in filt]
        right = [side(*x) for x in read_tiles(grad_ref, where)]
        for b in range(blocks):
            write_tile(
                back_ref, where, b, multiply_conj([(left[j], right[b + j]) for j in range(blocks - b)])
            )
        return carry

    lax.fori_loop(0, BLOCK // TILE * 2, tile, 0)
    stores = []
    for block in range(blocks):
        for signal, prod_ref in enumerate((conv_ref, back_ref)):
            invert_block(inverse_ref, prod_ref, out_ref, block, slots, signal)
        stores.append(send_run(out_ref, out_hbm, out_sem, slots, block, together))
    for copy in stores:
        copy.wait()


def final_kernel(
    ret_ref, k_ref, v_ref, u_ref, dq_hbm, dk_hbm, dv_hbm, dq_ref, dk_ref, dv_ref, out_sem, *, slots
):
    half_rows = ret_ref.shape[2]
    width = k_ref.shape[1] // CHUNKS
    count = width // BLOCK
    targets = ((dq_ref, dq_hbm), (dk_ref, dk_hbm), (dv_ref, dv_hbm))
    stores = [load_chunk(targets, out_sem, chunk, width) for chunk in range(CHUNKS)]
    for chunk in range(CHUNKS):
        for block in range(chunk * count, (chunk + 1) * count):
            for pair in range(2):
                lanes = pl.ds((block * 2 + pair) * LANES, LANES)
                conv, back = (
                    swap_halves(
                        *(ret_ref[slots[2 * pair + odd][block], signal] for odd in range(2))
                    )
                    for signal in range(2)
                )
                for part in range(2):
                    rows = pl.ds(part * half_rows, half_rows)
                    dq_ref[rows, lanes] = (u_ref[rows, lanes].astype(F32) * conv[part].astype(F32)).astype(BF16)
                    dk_ref[rows, lanes] = (back[part].astype(F32) * v_ref[rows, lanes].astype(F32)).astype(BF16)
                    dv_ref[rows, lanes] = (back[part].astype(F32) * k_ref[rows, lanes].astype(F32)).astype(BF16)
        for copy in stores[chunk]:
            copy.start()
    for row in stores:
        for copy in row:
            copy.wait()


def spread_kernel(
    place_ref, own_ref, up_ref, down_ref, far_ref, after_ref,
    out_hbm, held_ref, out_ref, out_sem, *, scale
):
    count = held_ref.shape[0]
    rows = held_ref.shape[1]
    step = rows // SPREAD_CHUNKS
    place = place_ref[0]
    for ref, shift in ((own_ref, 0), (up_ref, 1), (down_ref, 3), (far_ref, 2)):
        held_ref[lax.rem(place + count - shift, count)] = ref[...]
    stores = []
    for chunk in range(SPREAD_CHUNKS):
        part = pl.ds(chunk * step, step)
        for pair in range(2):
            lanes = pl.ds(pair * LANES, LANES)
            values = swap_halves(held_ref[2 * pair, part], held_ref[2 * pair + 1, part])
            for half in range(2):
                out_ref[pl.ds(half * rows + chunk * step, step), lanes] = values[half].astype(F32) * scale
        for half in range(2):
            part = pl.ds(half * rows + chunk * step, step)
            copy = pltpu.make_async_copy(out_ref.at[part], out_hbm.at[part], out_sem.at[half, chunk])
            copy.start()
            stores.append(copy)
    for copy in stores:
        copy.wait()


def local(queries, keys_in, value_in, upstream, filter_taps, *, ctx_count, seq_count):
    tokens, channels = queries.shape[1], queries.shape[2]
    length = filter_taps.shape[0]
    blocks = length // BLOCK
    y_count = 4
    z_count = seq_count // y_count
    half_rows = tokens // 2
    tokens_in = [a.reshape(tokens, channels) for a in (queries, keys_in, value_in, upstream)]
    params = pltpu.CompilerParams(vmem_limit_bytes=VMEM_LIMIT)
    upper, lower, inverse = (jnp.asarray(t) for t in dft_tables())
    members = y_count * ctx_count
    order = member_order(y_count, ctx_count, BLOCK // tokens)
    groups = [[z * members + m for m in order] for z in range(z_count)]
    place_of = [[order.index(y * ctx_count + c) for c in range(ctx_count)] for y in range(y_count)]
    hbm = pl.BlockSpec(memory_space=pltpu.HBM)
    whole = pl.BlockSpec(memory_space=pltpu.VMEM)
    scalars = pl.BlockSpec(memory_space=pltpu.SMEM)
    token_tile = pltpu.VMEM((tokens, channels), BF16)
    packed_shape = (members, 2, half_rows, LANES)

    packed = pl.pallas_call(
        functools.partial(gate_kernel, slots=place_of),
        in_specs=[hbm] * 4,
        out_specs=hbm,
        out_shape=pltpu.HBM(packed_shape, BF16),
        scratch_shapes=[token_tile] * 4
        + [
            pltpu.VMEM(packed_shape, BF16),
            pltpu.SemaphoreType.DMA((4, CHUNKS)),
            pltpu.SemaphoreType.DMA((blocks,)),
        ],
        compiler_params=params,
        name="gate",
    )(*(pltpu.with_memory_space_constraint(a, pltpu.HBM) for a in tokens_in))

    def exchange(array):
        return lax.all_to_all(array, ("seq", "ctx"), 0, 0, tiled=True, axis_index_groups=groups)

    arrived = exchange(packed)

    place = lax.rem(lax.axis_index("seq"), y_count).astype(jnp.int32).reshape(1)
    filt = pl.pallas_call(
        filter_kernel,
        grid_spec=pltpu.PrefetchScalarGridSpec(
            num_scalar_prefetch=1,
            grid=(1,),
            in_specs=[
                pl.BlockSpec((length, LANES), lambda i, place: (0, place[0] // 2)),
                pl.BlockSpec((2 * BLOCK, BLOCK), lambda i, place: (0, 0)),
                pl.BlockSpec((2 * BLOCK, BLOCK), lambda i, place: (0, 0)),
            ],
            out_specs=pl.BlockSpec((2, blocks, BLOCK, LANES), lambda i, place: (0, 0, 0, 0)),
        ),
        out_shape=pltpu.HBM((2, blocks, BLOCK, LANES), F32),
        compiler_params=params,
        name="filter_spectra",
    )(place, filter_taps, upper, lower)
    filt = pltpu.with_memory_space_constraint(filt, pltpu.HBM)

    signal_tile = pltpu.VMEM((blocks, BLOCK, 2 * LANES), BF16)
    product_tile = pltpu.VMEM((blocks, 2 * BLOCK, 2 * LANES), BF16)
    spectrum_shape = jax.ShapeDtypeStruct((blocks, 2 * BLOCK, 2 * LANES), F32)
    part_grad, value_spec, grad_spec, filt = pl.pallas_call(
        functools.partial(cross_kernel, slots=place_of),
        in_specs=[whole] * 3 + [hbm],
        out_specs=[whole] * 4,
        out_shape=[
            jax.ShapeDtypeStruct((length // 2, LANES), BF16),
            spectrum_shape,
            spectrum_shape,
            jax.ShapeDtypeStruct(filt.shape, F32),
        ],
        scratch_shapes=[
            signal_tile,
            pltpu.VMEM((blocks // 2, 2 * BLOCK, 2 * LANES), BF16),
            pltpu.SemaphoreType.DMA((2, blocks)),
        ],
        compiler_params=params,
        name="filter_terms",
    )(arrived, upper, inverse, filt)
    outgoing = pl.pallas_call(
        functools.partial(conv_kernel, slots=place_of),
        in_specs=[whole] * 4,
        out_specs=hbm,
        out_shape=pltpu.HBM(packed_shape, BF16),
        scratch_shapes=[
            product_tile,
            product_tile,
            pltpu.VMEM(packed_shape, BF16),
            pltpu.SemaphoreType.DMA((blocks,)),
        ],
        compiler_params=params,
        name="convolve",
    )(value_spec, grad_spec, filt, inverse)
    swapped = lax.ppermute(
        part_grad, "seq", [(s, (s + y_count) % seq_count) for s in range(seq_count)]
    )
    summed = (part_grad.astype(F32) + swapped.astype(F32)).astype(BF16)
    outgoing, summed = lax.optimization_barrier((outgoing, summed))
    others = [
        lax.ppermute(
            summed,
            "seq",
            [(s, s // y_count * y_count + (s + shift) % y_count) for s in range(seq_count)],
        )
        for shift in (1, 3, 2)
    ]
    returned = exchange(outgoing)
    query_grad, key_grad, value_grad = pl.pallas_call(
        functools.partial(final_kernel, slots=place_of),
        in_specs=[whole] * 4,
        out_specs=[hbm] * 3,
        out_shape=[pltpu.HBM((tokens, channels), BF16)] * 3,
        scratch_shapes=[token_tile] * 3 + [pltpu.SemaphoreType.DMA((3, CHUNKS))],
        compiler_params=pltpu.CompilerParams(vmem_limit_bytes=SMALL_LIMIT),
        name="products",
    )(returned, *tokens_in[1:])
    filter_grad = pl.pallas_call(
        functools.partial(spread_kernel, scale=1.0 / math.sqrt(length * seq_count)),
        in_specs=[scalars] + [whole] * 4 + [hbm],
        out_specs=hbm,
        out_shape=pltpu.HBM((length, 2 * LANES), F32),
        scratch_shapes=[
            pltpu.VMEM((y_count, length // 2, LANES), BF16),
            pltpu.VMEM((length, 2 * LANES), F32),
            pltpu.SemaphoreType.DMA((2, SPREAD_CHUNKS)),
        ],
        compiler_params=pltpu.CompilerParams(vmem_limit_bytes=SMALL_LIMIT),
        name="spread",
    )(place, summed, *others, pltpu.with_memory_space_constraint(query_grad, pltpu.HBM))
    return (
        query_grad.reshape(queries.shape),
        key_grad.reshape(queries.shape),
        value_grad.reshape(queries.shape),
        filter_grad,
    )


def solution(mesh):
    return jax.shard_map(
        functools.partial(local, ctx_count=mesh.shape["ctx"], seq_count=mesh.shape["seq"]),
        mesh=mesh,
        in_specs=(
            P("seq", "ctx", None),
            P("seq", "ctx", None),
            P("seq", "ctx", None),
            P("seq", "ctx", None),
            P(None, "ctx"),
        ),
        out_specs=(
            P("seq", "ctx", None),
            P("seq", "ctx", None),
            P("seq", "ctx", None),
            P(None, "ctx"),
        ),
        check_vma=False,
    )
```
